128 devices in a mesh: slab: 8 (over y, core), cross: 16 (over x, z).
Axes of the slice: x: 4, y: 4, z: 4, core: 2. Of those that a mesh axis runs over, the one named last changes fastest.
Arguments:
- state: float32 [22, 512, 4096], P(None, ('slab', 'cross')), may hold values from -6 to 6
- velocity: float32 [3, 512, 4096], P(None, ('slab', 'cross')), may hold values from -3 to 3
- history: float32 [22, 512, 4096], P(None, ('slab', 'cross')), may hold values from -6 to 6
- diffusion: float32 [22], replicated, may hold values from 0.05 to 0.5
- box_target: int32 [8, 64], P('slab', 'cross'), may hold values from 0 to 63, as said below
- parcel_mass: float32 [524288], P(('slab', 'cross')), may hold values from 0.2 to 2
- parcel_state: float32 [5, 524288], P(None, ('slab', 'cross')), may hold values from -6 to 6
- parcel_box: int32 [524288], P(('slab', 'cross')), may hold values from 0 to 511, as said below
- parcel_cell: int32 [524288], P(('slab', 'cross')), may hold values from 0 to 4095
- parcel_count: int32 [128], P(('slab', 'cross')), may hold values from 1024 to 4096, as said below
Outputs:
- new_state: float32 [22, 512, 4096], P(None, ('slab', 'cross'))
- tendency: float32 [22, 512, 4096], P(None, ('slab', 'cross'))
The draws below stay inside these ranges and needn't reach their ends.
Inputs may be any that keep to these rules, and one draw needn't show every extreme that they name: `box_target`: within each slab group every new owner and slot receives exactly one box, and the 4 boxes of one device go to 4 different owners. The owner device is parcel_box // 4. On each device the parcels of one owner stand together. At most 64 parcels of one device go to one owner, and some owner receives 64 live parcels from every device. `parcel_count`: A multiple of 128; parcels below the count are live, the others are padding; some device is full.
All inputs are finite; a program needn't handle non-finite values.
Results may differ from the reference program's by a relative error of at most 0.000082.
Values sent between devices are 32-bit elements; how exact they have to be, the bound alone decides.
A program may use at most 192 MiB of HBM per device.

```python
import math
import jax
import jax.numpy as jnp
from jax import lax

BE = 16
PAR_DEV = 4096
BOX_DEV = 4
FIELDS = 22
CELLS = 4096
BOXES = 512
PARCELS = 524288
N_SLAB = 8
N_CROSS = 16


def random_order(key, rows, width):
    rank_loads = jax.random.randint(key, (rows, width), 0, 1 << 20) * width + jnp.arange(width, dtype=jnp.int32)[None, :]
    return jnp.argsort(rank_loads, axis=1).astype(jnp.int32)


def draw_box_target(key, part):
    sorting_labels = jax.random.split(key, 4)
    offsets = random_order(sorting_labels[0], N_SLAB, N_CROSS)[:, :BOX_DEV]
    mixing = random_order(sorting_labels[1], N_SLAB, N_CROSS)
    labels = random_order(sorting_labels[2], N_SLAB, N_CROSS)
    new_slot = random_order(sorting_labels[3], N_SLAB * N_CROSS, BOX_DEV).reshape(N_SLAB, N_CROSS * BOX_DEV)
    chosen = jnp.take_along_axis(offsets, new_slot, axis=1).reshape(N_SLAB, N_CROSS, BOX_DEV)
    position = ((labels[:, :, None] + chosen) % N_CROSS).reshape(N_SLAB, N_CROSS * BOX_DEV)
    owner = jnp.take_along_axis(mixing, position, axis=1)
    return (owner * BOX_DEV + new_slot).astype(jnp.int32)


def draw_parcel_box(key, part):
    process_total = N_SLAB * N_CROSS
    limit = 2 * PAR_DEV // process_total
    sorting_labels = jax.random.split(key, 5)
    hottest_region_index = jax.random.randint(sorting_labels[0], (), 0, process_total)
    hottest_regions = jax.random.randint(sorting_labels[1], (process_total,), 0, 16) == 0
    lightest_rank = jnp.arange(process_total, dtype=jnp.int32)
    surplus_weight = jnp.where(lightest_rank == hottest_region_index, 1 << 14, jnp.where(hottest_regions, 2048, 0))
    unscaled_scores = jax.random.randint(sorting_labels[2], (process_total, process_total), 0, 4096)
    rank_loads = (unscaled_scores + surplus_weight[None, :]) * process_total + lightest_rank[None, :]
    ranking = jnp.argsort(-rank_loads, axis=1).astype(jnp.int32)
    lengths = jax.random.randint(sorting_labels[3], (process_total, process_total), limit // 2, limit + 1)
    lengths = lengths.at[:, 0].set(limit)
    ends = jnp.cumsum(lengths, axis=1)
    position = jnp.arange(PAR_DEV, dtype=jnp.int32)
    segment = jax.vmap(lambda row: jnp.searchsorted(row, position, side='right'))(ends).astype(jnp.int32)
    target = jnp.take_along_axis(ranking, segment, axis=1)
    slot = jax.random.randint(sorting_labels[4], (process_total, PAR_DEV), 0, BOX_DEV)
    return (target * BOX_DEV + slot).reshape(-1).astype(jnp.int32)


def draw_parcel_count(key, part):
    process_total = N_SLAB * N_CROSS
    sorting_labels = jax.random.split(key, 2)
    blocks = jax.random.randint(sorting_labels[0], (process_total,), PAR_DEV // 512, PAR_DEV // 128 + 1)
    heaviest_rank = jax.random.randint(sorting_labels[1], (), 0, process_total)
    blocks = jnp.where(jnp.arange(process_total) == heaviest_rank, PAR_DEV // 128, blocks)
    return (blocks * 128).astype(jnp.int32)


def set_ends(values, key, least, high):
    longest = values.shape.index(max(values.shape))
    spots = []
    for shift in (0, 1):
        where = [jax.random.randint(jax.random.fold_in(key, axis), (), 0, length) for axis, length in enumerate(values.shape)]
        where[longest] = (where[longest] + shift) % values.shape[longest]
        spots.append(tuple(where))
    return values.at[spots[0]].set(least).at[spots[1]].set(high)


def steps_of(stream_key, extent, cuts, low, high):
    gain, own = 1.0, jax.random.fold_in(stream_key, 6)
    for axis_at, blocks in cuts:
        steps = jnp.exp(jax.random.uniform(jax.random.fold_in(own, axis_at), (blocks,), jnp.float32, low / len(cuts), high / len(cuts)))
        gain = gain * jnp.repeat(steps, extent[axis_at] // blocks).reshape([-1 if axis == axis_at else 1 for axis in range(len(extent))])
    return gain


def bell_draw(key, shape, scale, bound, cuts=(), kind=jnp.bfloat16):
    result = scale * jax.random.normal(key, shape, jnp.float32)
    if cuts:
        result = result * steps_of(key, shape, cuts, -0.22, 0.18)
    return jnp.clip(result, -bound, bound).astype(kind)


def setup_inputs(seed: int = 0) -> dict:
    key_list = jax.random.split(jax.random.key(seed), 11)
    return {
        "state": bell_draw(key_list[0], (FIELDS, BOXES, CELLS), 1.0, 6.0, ((1, 128),), jnp.float32),
        "velocity": bell_draw(key_list[1], (3, BOXES, CELLS), 0.5, 3.0, ((1, 128),), jnp.float32),
        "history": bell_draw(key_list[2], (FIELDS, BOXES, CELLS), 1.0, 6.0, ((1, 128),), jnp.float32),
        "diffusion": jnp.clip(jnp.exp(jax.random.uniform(key_list[3], (FIELDS,), jnp.float32, math.log(0.05), math.log(0.5))), 0.05, 0.5),
        "box_target": draw_box_target(jax.random.fold_in(key_list[10], 71), 0),
        "parcel_mass": jnp.clip(jnp.exp(math.log(2.0) - 2.3025851 * jax.random.uniform(key_list[5], (PARCELS,), jnp.float32) ** steps_of(key_list[5], (PARCELS,), ((0, 128),), -0.2, 0.2)), 0.2, 2.0),
        "parcel_state": bell_draw(key_list[6], (5, PARCELS), 1.0, 6.0, ((1, 128),), jnp.float32),
        "parcel_box": draw_parcel_box(jax.random.fold_in(key_list[10], 71), 0),
        "parcel_cell": set_ends(jax.random.randint(key_list[8], (PARCELS,), 0, CELLS), jax.random.fold_in(key_list[8], 1), 0, CELLS - 1).astype(jnp.int32),
        "parcel_count": draw_parcel_count(jax.random.fold_in(key_list[10], 71), 0),
    }


TIME_STEP = 0.2
LATENT = 0.5
DEPOSIT = 0.25

def to_grid(boxes):
    count = boxes.shape[0]
    shaped = boxes.reshape(count, N_SLAB, N_CROSS, BOX_DEV, BE, BE, BE)
    return shaped.transpose(0, 2, 4, 1, 5, 3, 6).reshape(count, BE * N_CROSS, BE * N_SLAB, BE * BOX_DEV)

def from_grid(grid):
    count = grid.shape[0]
    shaped = grid.reshape(count, N_CROSS, BE, N_SLAB, BE, BOX_DEV, BE)
    return shaped.transpose(0, 3, 1, 5, 2, 4, 6).reshape(count, BOXES, CELLS)

def face_flux(coeff, low_q, high_q, low_g, high_g, low_u, high_u):
    return coeff * (0.5 * (low_g + high_g)) * (high_q - low_q) - 0.5 * (low_u + high_u) * (0.5 * (low_q + high_q))

def field_tendency(field, coeff, spread, flow):
    flux_x = face_flux(coeff, field[:-1], field[1:], spread[:-1], spread[1:], flow[0, :-1], flow[0, 1:])
    padded_x = jnp.pad(flux_x, ((1, 1), (0, 0), (0, 0)))
    total = padded_x[1:] - padded_x[:-1]
    flux_z = face_flux(coeff, field, jnp.roll(field, -1, axis=1), spread, jnp.roll(spread, -1, axis=1), flow[2], jnp.roll(flow[2], -1, axis=1))
    total = total + flux_z - jnp.roll(flux_z, 1, axis=1)
    flux_y = face_flux(coeff, field[:, :, :-1], field[:, :, 1:], spread[:, :, :-1], spread[:, :, 1:], flow[1, :, :, :-1], flow[1, :, :, 1:])
    padded_y = jnp.pad(flux_y, ((0, 0), (0, 0), (1, 1)))
    return total + padded_y[:, :, 1:] - padded_y[:, :, :-1]

def reference(state, velocity, history, diffusion, box_target, parcel_mass, parcel_state, parcel_box, parcel_cell, parcel_count):
    slab_index = jnp.arange(N_SLAB, dtype=jnp.int32)[:, None]
    new_index = ((slab_index * N_CROSS + box_target // BOX_DEV) * BOX_DEV + box_target % BOX_DEV).reshape(-1).astype(jnp.int32)
    placed_state = jnp.zeros_like(state).at[:, new_index].set(state)
    placed_velocity = jnp.zeros_like(velocity).at[:, new_index].set(velocity)
    placed_history = jnp.zeros_like(history).at[:, new_index].set(history)
    grid_state = to_grid(placed_state)
    grid_flow = to_grid(placed_velocity)
    spread = 1.0 + 0.5 * jnp.tanh(grid_state[FIELDS - 1])

    def one_field(pair):
        return field_tendency(pair[0], pair[1], spread, grid_flow)
    tendency = from_grid(lax.map(one_field, (grid_state, diffusion)))
    advanced = placed_state + TIME_STEP * (1.5 * tendency - 0.5 * placed_history)
    position = jnp.arange(PARCELS, dtype=jnp.int32)
    live = position % PAR_DEV < parcel_count[position // PAR_DEV]
    flat_index = (parcel_box * CELLS + parcel_cell).astype(jnp.int32)
    fuel = advanced[0].reshape(-1)[flat_index]
    energy = advanced[FIELDS - 1].reshape(-1)[flat_index]
    gas_flow = placed_velocity.reshape(3, -1)[:, flat_index]
    slip = lax.optimization_barrier(jnp.sum((gas_flow - parcel_state[2:5]) ** 2, axis=0))
    coef = jnp.where(live, parcel_mass * jnp.sqrt(1.0 + slip), jnp.float32(0.0))
    rate = coef * (parcel_state[0] - fuel)
    heat = coef * (parcel_state[1] - energy) - LATENT * rate
    fuel_source = jnp.zeros((BOXES * CELLS,), jnp.float32).at[flat_index].add(rate)
    heat_source = jnp.zeros((BOXES * CELLS,), jnp.float32).at[flat_index].add(heat)
    new_state = advanced.at[0].add(DEPOSIT * fuel_source.reshape(BOXES, CELLS))
    new_state = new_state.at[FIELDS - 1].add(DEPOSIT * heat_source.reshape(BOXES, CELLS))
    return (new_state, tendency)
```

```python
import functools

import jax
import jax.numpy as jnp
from jax import lax
from jax.experimental import pallas as pl
from jax.experimental.pallas import tpu as pltpu
from jax.sharding import PartitionSpec as P

MESH = pl.DeviceIdType.MESH
F32 = jnp.float32
BF16 = jnp.bfloat16

BE = 16
PAR_DEV = 4096
CAP = 64
FIELDS = 22
N_SLAB = 8
N_CROSS = 16
CHUNK = 512

TIME_STEP = 0.2
LATENT = 0.5
DEPOSIT = 0.25

GROUPS = (
    ((1, 0, 3), (0, 0, 10)),
    ((0, 10, 12),),
    ((2, 0, 11),),
    ((2, 11, 11),),
)
WIDTHS = (13, 12, 11, 11)


def iota(dim, shape=(8, 128)):
    return lax.broadcasted_iota(jnp.int32, shape, dim)


def lane_roll(x, shift):
    shift = shift % 128
    return x if shift == 0 else pltpu.roll(x, shift, x.ndim - 1)


def sub_roll(x, shift):
    shift = shift % 8
    return x if shift == 0 else pltpu.roll(x, shift, x.ndim - 2)


def pack_kernel(start_ref, len_ref, w_ref, out_ref):
    lane = iota(1)
    row = iota(0)

    def body(o, carry):
        start = start_ref[o]
        base = pl.multiple_of((start // 128) * 128, 128)
        window = w_ref[:, pl.ds(base, 256)]
        window = pltpu.roll(window, 256 - (start - base), 1)[:, :128]
        window = jnp.where((row == 0) & (lane >= len_ref[o]), 0.0, window)
        low = window[0:4]
        high = pltpu.roll(window, 64, 1)[4:8]
        out_ref[o % N_CROSS, o // N_CROSS] = jnp.where(lane[0:4] < 64, low, high)
        return carry

    lax.fori_loop(0, N_SLAB * N_CROSS, body, 0, unroll=4)


def pack(start, length, w):
    return pl.pallas_call(
        pack_kernel,
        out_shape=jax.ShapeDtypeStruct((N_CROSS, N_SLAB, 4, 128), F32),
        in_specs=[
            pl.BlockSpec(memory_space=pltpu.SMEM),
            pl.BlockSpec(memory_space=pltpu.SMEM),
            pl.BlockSpec(memory_space=pltpu.VMEM),
        ],
        out_specs=pl.BlockSpec(memory_space=pltpu.VMEM),
    )(start, length, w)


def mix_kernel(*refs):
    (s_ref, v_ref, h_ref, tg_ref, sb_ref) = refs[:5]
    arrays = (s_ref, v_ref, h_ref)
    placed = refs[5:9]
    (xl, xh, zl, zh, z0, z15, r2) = refs[9:16]
    bufs = refs[16:20]
    outs = refs[20:24]
    (tgb, inv_v, inv_s, r1) = refs[24:28]
    (tsem, p1, p2, hsem, psem, lsem) = refs[28:34]

    me_s = lax.axis_index("slab")
    me_c = lax.axis_index("cross")

    def cross(d):
        return lax.rem(me_c + d, N_CROSS)

    def slab(d):
        return lax.rem(me_s + d, N_SLAB)

    barrier = pltpu.get_barrier_semaphore()

    def greet_c(d, carry):
        pl.semaphore_signal(barrier, inc=1, device_id=(me_s, cross(d)), device_id_type=MESH)
        return carry

    def greet_s(d, carry):
        pl.semaphore_signal(barrier, inc=1, device_id=(slab(d), me_c), device_id_type=MESH)
        return carry

    lax.fori_loop(1, N_CROSS, greet_c, 0)
    lax.fori_loop(1, N_SLAB, greet_s, 0)
    pl.semaphore_wait(barrier, N_CROSS - 1 + N_SLAB - 1)

    def remote(src, dst, sems, peer):
        return pltpu.make_async_remote_copy(
            src_ref=src,
            dst_ref=dst,
            send_sem=sems.at[0],
            recv_sem=sems.at[1],
            device_id=peer,
            device_id_type=MESH,
        )

    def drain(ref, sem):
        pltpu.make_async_copy(ref, ref, sem).wait()

    def send_targets(d, carry):
        remote(tg_ref, tgb.at[me_c], tsem, (me_s, cross(d))).start()
        return carry

    lax.fori_loop(1, N_CROSS, send_targets, 0)
    tgb[me_c] = tg_ref[...]

    def parts(g):
        at = 0
        for which, first, count in GROUPS[g]:
            yield arrays[which], first, count, at
            at += count

    def phase1(g):
        sems = p1.at[g]

        def body(d, carry):
            m = cross(d)
            for src, first, count, at in parts(g):
                remote(
                    src.at[pl.ds(first, count), m],
                    bufs[g].at[me_c, pl.ds(at, count)],
                    sems,
                    (me_s, m),
                ).start()
            return carry

        lax.fori_loop(1, N_CROSS, body, 0)
        for src, first, count, at in parts(g):
            pltpu.make_async_copy(
                src.at[pl.ds(first, count), me_c], bufs[g].at[me_c, pl.ds(at, count)], lsem.at[g]
            ).start()

    def phase2(g):
        width = WIDTHS[g]
        sems = p1.at[g]
        drain(bufs[g].at[pl.ds(0, N_CROSS - 1)], sems.at[1])
        drain(bufs[g].at[0], lsem.at[g])

        def fill(t):
            for q in range(4):
                code = inv_s[t * 4 + q, 0] & 63
                outs[g][t, :, q : q + 5 : 4, :] = bufs[g][
                    lax.div(code, 4), :, pl.ds(lax.rem(code, 4), 2, stride=4), :
                ]

        def body(d, carry):
            t = cross(d)
            fill(t)
            remote(outs[g].at[t], placed[g].at[me_c], p2.at[g], (me_s, t)).start()
            return carry

        lax.fori_loop(1, N_CROSS, body, 0)
        fill(me_c)
        pltpu.make_async_copy(outs[g].at[me_c], placed[g].at[me_c], lsem.at[g]).start()

    def landed(g):
        drain(placed[g].at[pl.ds(0, N_CROSS - 1)], p2.at[g, 1])
        drain(placed[g].at[0], lsem.at[g])

    def sent(g):
        drain(bufs[g].at[pl.ds(0, N_CROSS - 1)], p1.at[g, 0])
        drain(outs[g].at[pl.ds(0, N_CROSS - 1)], p2.at[g, 0])

    phase1(0)
    phase1(1)

    drain(tgb.at[pl.ds(0, N_CROSS - 1)], tsem.at[1])
    flat = tgb[0]
    for s in range(1, N_CROSS):
        flat = flat + tgb[s]
    for tile in range(8):
        hit = flat == iota(0) + 8 * tile
        code = jnp.sum(jnp.where(hit & (iota(1) < 64), iota(1).astype(F32), 0.0), axis=1, keepdims=True)
        inv_v[8 * tile : 8 * tile + 8, :] = jnp.broadcast_to(code, (8, 128)).astype(jnp.int32)
    to_scalar = pltpu.make_async_copy(inv_v, inv_s, lsem.at[4])
    to_scalar.start()
    to_scalar.wait()

    phase2(0)

    def parcels1(d, carry):
        c = cross(d)
        remote(sb_ref.at[c], r1.at[me_c], psem.at[0], (me_s, c)).start()
        return carry

    lax.fori_loop(1, N_CROSS, parcels1, 0)
    own = pltpu.make_async_copy(sb_ref.at[me_c], r1.at[me_c], lsem.at[4])
    own.start()
    phase1(2)
    phase2(1)
    phase1(3)

    own.wait()
    drain(r1.at[pl.ds(0, N_CROSS - 1)], psem.at[0, 1])

    def parcels2(d, carry):
        a = slab(d)
        remote(r1.at[:, a], r2.at[me_s], psem.at[1], (a, me_c)).start()
        return carry

    lax.fori_loop(1, N_SLAB, parcels2, 0)
    own = pltpu.make_async_copy(r1.at[:, me_s], r2.at[me_s], lsem.at[4])
    own.start()

    landed(0)
    landed(1)
    x_lo = (me_s, cross(N_CROSS - 1))
    x_hi = (me_s, cross(1))
    halo = []
    for g in range(2):
        at = pl.ds(sum(WIDTHS[:g]), WIDTHS[g])
        halo.append(remote(placed[g].at[0], xh.at[at], hsem.at[g], x_lo))
        halo.append(remote(placed[g].at[BE - 1], xl.at[at], hsem.at[2 + g], x_hi))
    for copy in halo:
        copy.start()
    pack_z(placed, z0, z15)
    z_lo = (slab(N_SLAB - 1), me_c)
    z_hi = (slab(1), me_c)
    for copy in (remote(z0, zh, hsem.at[4], z_lo), remote(z15, zl, hsem.at[5], z_hi)):
        copy.start()
        halo.append(copy)

    phase2(2)
    phase2(3)
    for copy in halo:
        copy.wait()
    own.wait()
    drain(r2.at[pl.ds(0, N_SLAB - 1)], psem.at[1, 1])
    landed(2)
    landed(3)

    drain(tgb.at[pl.ds(0, N_CROSS - 1)], tsem.at[0])
    drain(r1.at[pl.ds(0, N_CROSS - 1)], psem.at[0, 0])
    drain(r2.at[pl.ds(0, N_SLAB - 1)], psem.at[1, 0])
    for g in range(4):
        sent(g)


def pack_z(placed, z0, z15):
    lane16 = iota(1) // 16
    upper = iota(0) >= 4

    for g in range(2):
        first = sum(WIDTHS[:g])

        def body(f, carry):
            low = [None, None]
            high = [None, None]
            for ih in range(2):
                for il in range(8):
                    x = placed[g][ih * 8 + il, f]
                    a = lane_roll(x, 16 * il)
                    b = lane_roll(x, 16 * il + 16)
                    if il == 0:
                        low[ih], high[ih] = a, b
                    else:
                        low[ih] = jnp.where(lane16 == il, a, low[ih])
                        high[ih] = jnp.where(lane16 == il, b, high[ih])
            z0[first + f] = jnp.where(upper, sub_roll(low[1], 4), low[0])
            z15[first + f] = jnp.where(upper, high[1], sub_roll(high[0], 4))
            return carry

        lax.fori_loop(0, WIDTHS[g], body, 0)


def mix(state, velocity, history, targets, sendbuf):
    vm = pl.BlockSpec(memory_space=pltpu.VMEM)
    hbm = pl.BlockSpec(memory_space=pl.ANY)
    total = WIDTHS[0] + WIDTHS[1]
    group = [(N_CROSS, w, 8, 128) for w in WIDTHS]
    outs = group + [(total, 8, 128)] * 6 + [(N_SLAB, N_CROSS, 4, 128)]
    return pl.pallas_call(
        mix_kernel,
        out_shape=[jax.ShapeDtypeStruct(s, F32) for s in outs],
        in_specs=[hbm, hbm, hbm, vm, vm],
        out_specs=[vm] * len(outs),
        scratch_shapes=[pltpu.VMEM(s, F32) for s in group + group]
        + [
            pltpu.VMEM((N_CROSS, 8, 128), jnp.int32),
            pltpu.VMEM((64, 128), jnp.int32),
            pltpu.SMEM((64, 128), jnp.int32),
            pltpu.VMEM((N_CROSS, N_SLAB, 4, 128), F32),
            pltpu.SemaphoreType.DMA((2,)),
            pltpu.SemaphoreType.DMA((4, 2)),
            pltpu.SemaphoreType.DMA((4, 2)),
            pltpu.SemaphoreType.DMA((6, 2)),
            pltpu.SemaphoreType.DMA((2, 2)),
            pltpu.SemaphoreType.DMA((5,)),
        ],
        compiler_params=pltpu.CompilerParams(
            collective_id=0, has_side_effects=True, vmem_limit_bytes=40 * 2**20
        ),
    )(state, velocity, history, targets, sendbuf)


def spread_of(e):
    return 1.0 + 0.5 * jnp.tanh(e)


def finish_kernel(
    d_ref, p0, p1, p2, p3, xl, xh, zl, zh, z0, z15, r2, new_ref, tend_ref,
    gx, hx, gy, hy, gz, hz, gzp, hzp, vals, tabs,
):
    me_c = lax.axis_index("cross")
    lane = iota(1)
    row = iota(0)
    kl7 = lane >= 112
    kl0 = lane < 16
    top = kl7 & (row >= 4)
    bottom = kl0 & (row < 4)
    j15 = lane % 16 == 15
    j0 = lane % 16 == 0
    wall_y = j15 & (row % 4 == 3)

    def up_z(q):
        return lane_roll(jnp.where(kl0, sub_roll(q, 4), q), -16)

    def down_z(q):
        return lane_roll(jnp.where(kl7, sub_roll(q, 4), q), 16)

    def up_y(q):
        return jnp.where(j15, sub_roll(lane_roll(q, 15), -1), lane_roll(q, -1))

    def down_y(q):
        return jnp.where(j0, sub_roll(lane_roll(q, -15), 1), lane_roll(q, 1))

    def put_top(packed, i):
        ih, il = divmod(i, 8)
        return lane_roll(packed[1 - ih], 112 - 16 * il)

    def put_bottom(packed, i):
        ih, il = divmod(i, 8)
        return lane_roll(packed[ih], -16 * il)

    E = WIDTHS[1] - 1
    EH = WIDTHS[0] + WIDTHS[1] - 1
    first_wall = jnp.where(me_c == 0, 0.0, 1.0)
    last_wall = jnp.where(me_c == N_CROSS - 1, 0.0, 1.0)
    before_g = spread_of(xl[EH])
    before_u = xl[0]
    for i in range(BE + 1):
        if i < BE:
            now_g, now_u = spread_of(p1[i, E]), p0[i, 0]
        else:
            now_g, now_u = spread_of(xh[EH]), xh[0]
        g, h = 0.5 * (before_g + now_g), 0.25 * (before_u + now_u)
        if i == 0:
            g, h = g * first_wall, h * first_wall
        if i == BE:
            g, h = g * last_wall, h * last_wall
        gx[i], hx[i] = g, h
        before_g, before_u = now_g, now_u
        if i < BE:
            uy, uz = p0[i, 1], p0[i, 2]
            gy[i] = jnp.where(wall_y, 0.0, 0.5 * (now_g + up_y(now_g)))
            hy[i] = jnp.where(wall_y, 0.0, 0.25 * (uy + up_y(uy)))
            gz[i] = 0.5 * (now_g + up_z(now_g))
            hz[i] = 0.25 * (uz + up_z(uz))
    gzp[0] = 0.5 * (spread_of(zl[EH]) + spread_of(z0[EH]))
    gzp[1] = 0.5 * (spread_of(z15[EH]) + spread_of(zh[EH]))
    hzp[0] = 0.25 * (zl[2] + z0[2])
    hzp[1] = 0.25 * (z15[2] + zh[2])

    def flux(d, g, h, low, high):
        return (d * g) * (high - low) - h * (high + low)

    def transport(q_ref, h_ref, q_at, x_at, h_at, out_at, count):
        def body(n, carry):
            f = out_at + n
            d = d_ref[f]
            xf = x_at + n
            qf = q_at + n
            edge0 = flux(d, gzp[0], hzp[0], zl[xf], z0[xf])
            edge15 = flux(d, gzp[1], hzp[1], z15[xf], zh[xf])
            edge0 = (edge0, sub_roll(edge0, 4))
            edge15 = (edge15, sub_roll(edge15, 4))
            q = q_ref[0, qf]
            fx = flux(d, gx[0], hx[0], xl[xf], q)
            for i in range(BE):
                ahead = q_ref[i + 1, qf] if i < BE - 1 else xh[xf]
                fx_up = flux(d, gx[i + 1], hx[i + 1], q, ahead)
                total = fx_up - fx
                fz = flux(d, gz[i], hz[i], q, up_z(q))
                fz = jnp.where(top, put_top(edge15, i), fz)
                fz_low = jnp.where(bottom, put_bottom(edge0, i), down_z(fz))
                total = total + fz - fz_low
                fy = flux(d, gy[i], hy[i], q, up_y(q))
                total = total + fy - down_y(fy)
                tend_ref[f, i] = total
                old = h_ref[i, h_at + n]
                new_ref[f, i] = q + TIME_STEP * (1.5 * total - 0.5 * old)
                fx = fx_up
                q = ahead
            return carry

        lax.fori_loop(0, count, body, 0)

    transport(p0, p2, 3, 3, 0, 0, 10)
    transport(p1, p2, 0, 13, 10, 10, 1)
    transport(p1, p3, 1, 14, 0, 11, 11)

    tables = [new_ref[0], new_ref[FIELDS - 1]] + [p0[:, d] for d in range(3)]
    for n, table in enumerate(tables):
        table = table.reshape(128, 128)
        first = table.astype(BF16)
        tabs[128 * n : 128 * n + 128, 0:128] = first
        tabs[128 * n : 128 * n + 128, 128:256] = (table - first.astype(F32)).astype(BF16)

    half = iota(1, (4, 128)) < 64

    def unpack(n, carry):
        a, b = r2[n // 8, 2 * (n % 8)], r2[n // 8, 2 * (n % 8) + 1]
        at = pl.ds(pl.multiple_of(n * 128, 128), 128)
        vals[0:4, at] = jnp.where(half, a, pltpu.roll(b, 64, 1))
        vals[4:8, at] = jnp.where(half, pltpu.roll(a, 64, 1), b)
        return carry

    lax.fori_loop(0, 64, unpack, 0, unroll=4)

    number = lax.broadcasted_iota(jnp.int32, (128, CHUNK), 0).astype(F32)

    def deposit(n, acc):
        v = vals[:, pl.ds(pl.multiple_of(n * CHUNK, CHUNK), CHUNK)]
        at_row = number == v[3:4]
        at_lane = jnp.where(number == v[7:8], 1.0, 0.0).astype(BF16)
        picked = jnp.dot(
            tabs[...], jnp.concatenate([at_lane, at_lane], axis=0), preferred_element_type=F32
        )

        def value(m):
            return jnp.sum(
                jnp.where(at_row, picked[128 * m : 128 * m + 128], 0.0), axis=0, keepdims=True
            )

        slip = (value(2) - v[4:5]) ** 2 + (value(3) - v[5:6]) ** 2 + (value(4) - v[6:7]) ** 2
        coef = v[0:1] * jnp.sqrt(1.0 + slip)
        rate = coef * (v[1:2] - value(0))
        heat = coef * (v[2:3] - value(1)) - LATENT * rate
        rows = []
        for x in (rate, heat):
            first = x.astype(BF16).astype(F32)
            rows.append(jnp.where(at_row, first, 0.0).astype(BF16))
            rows.append(jnp.where(at_row, x - first, 0.0).astype(BF16))
        return acc + lax.dot_general(
            jnp.concatenate(rows, axis=0),
            at_lane,
            (((1,), (1,)), ((), ())),
            preferred_element_type=F32,
        )

    acc = lax.fori_loop(
        0, N_SLAB * N_CROSS * CAP // CHUNK, deposit, jnp.zeros((512, 128), F32)
    )
    fuel = (acc[0:128] + acc[128:256]).reshape(BE, 8, 128)
    heat = (acc[256:384] + acc[384:512]).reshape(BE, 8, 128)
    new_ref[0] = new_ref[0] + DEPOSIT * fuel
    new_ref[FIELDS - 1] = new_ref[FIELDS - 1] + DEPOSIT * heat


def finish(diffusion, arrived):
    vm = pl.BlockSpec(memory_space=pltpu.VMEM)
    out = jax.ShapeDtypeStruct((FIELDS, BE, 8, 128), F32)
    return pl.pallas_call(
        finish_kernel,
        out_shape=[out, out],
        in_specs=[pl.BlockSpec(memory_space=pltpu.SMEM)] + [vm] * len(arrived),
        out_specs=[vm, vm],
        scratch_shapes=[pltpu.VMEM((BE + 1, 8, 128), F32)] * 2
        + [pltpu.VMEM((BE, 8, 128), F32)] * 4
        + [pltpu.VMEM((2, 8, 128), F32)] * 2
        + [
            pltpu.VMEM((8, N_SLAB * N_CROSS * CAP), F32),
            pltpu.VMEM((640, 256), BF16),
        ],
        compiler_params=pltpu.CompilerParams(vmem_limit_bytes=40 * 2**20),
    )(diffusion, *arrived)


def to_tiles(array):
    fields = array.shape[0]
    return (
        array.reshape(fields, 4, 32, 128).transpose(0, 2, 1, 3).reshape(fields, BE, 8, 128)
    )


def from_tiles(array):
    fields = array.shape[0]
    return array.reshape(fields, 32, 4, 128).transpose(0, 2, 1, 3).reshape(fields, 4, 4096)


def per_device(
    state,
    velocity,
    history,
    diffusion,
    box_target,
    parcel_mass,
    parcel_state,
    parcel_box,
    parcel_cell,
    parcel_count,
):
    position = jnp.arange(PAR_DEV, dtype=jnp.int32)
    owner = parcel_box // 4
    here = owner[None, :] == jnp.arange(N_SLAB * N_CROSS, dtype=jnp.int32)[:, None]
    start = jnp.min(jnp.where(here, position[None, :], PAR_DEV - 1), axis=1)
    length = jnp.sum((here & (position < parcel_count[0])[None, :]).astype(jnp.int32), axis=1)
    row = ((parcel_cell // 128) * 4 + parcel_box % 4).astype(F32)
    lane = (parcel_cell % 128).astype(F32)
    w = jnp.concatenate(
        [parcel_mass[None], parcel_state[0:2], row[None], parcel_state[2:5], lane[None]], axis=0
    )
    w = jnp.pad(w, ((0, 0), (0, 256)))
    sendbuf = pack(start, length, w)

    spot = jnp.arange(128, dtype=jnp.int32) - 4 * lax.axis_index("cross")
    targets = jnp.sum(
        jnp.where(spot[None, :] == jnp.arange(4, dtype=jnp.int32)[:, None], box_target[0][:, None], 0),
        axis=0,
    )
    targets = jnp.broadcast_to(targets[None, :], (8, 128))
    arrived = mix(to_tiles(state), to_tiles(velocity), to_tiles(history), targets, sendbuf)
    new_state, tendency = finish(diffusion, arrived)
    return from_tiles(new_state), from_tiles(tendency)


def solution(mesh):
    return jax.shard_map(
        per_device,
        mesh=mesh,
        in_specs=(
            P(None, ("slab", "cross"), None),
            P(None, ("slab", "cross"), None),
            P(None, ("slab", "cross"), None),
            P(),
            P("slab", "cross"),
            P(("slab", "cross")),
            P(None, ("slab", "cross")),
            P(("slab", "cross")),
            P(("slab", "cross")),
            P(("slab", "cross")),
        ),
        out_specs=(P(None, ("slab", "cross"), None), P(None, ("slab", "cross"), None)),
        check_vma=False,
    )
```

```python
import jax
import jax.numpy as jnp
from jax import lax
from jax.experimental import pallas as pl
from jax.experimental.pallas import tpu as pltpu
from jax.sharding import PartitionSpec as P

MESH = pl.DeviceIdType.MESH
F32 = jnp.float32
BF16 = jnp.bfloat16

BE = 16
PAR_DEV = 4096
CAP = 64
FIELDS = 22
N_SLAB = 8
N_CROSS = 16
CHUNK = 512
VMEM_LIMIT = 60 * 2**20

TIME_STEP = 0.2
LATENT = 0.5
DEPOSIT = 0.25

GROUPS = (
    ((1, 0, 3), (0, 0, 10)),
    ((0, 10, 12), (2, 0, 1), (2, 21, 1)),
    ((2, 1, 10),),
    ((2, 11, 10),),
)
WIDTHS = (13, 14, 10, 10)
HALO = (13, 12)


def iota(dim, shape=(8, 128)):
    return lax.broadcasted_iota(jnp.int32, shape, dim)


def lane_roll(x, shift):
    shift = shift % 128
    return x if shift == 0 else pltpu.roll(x, shift, x.ndim - 1)


def sub_roll(x, shift):
    shift = shift % 8
    return x if shift == 0 else pltpu.roll(x, shift, x.ndim - 2)


def pack(mass, parcels, box, cell, count, w, spans_v, spans_s, sem, out):
    def columns(n, carry):
        at = pl.ds(pl.multiple_of(n * 128, 128), 128)
        w[n, 0:1] = mass[:, at]
        w[n, 1:3] = parcels[0:2, at]
        w[n, 3:4] = ((cell[:, at] // 128) * 4 + box[:, at] % 4).astype(F32)
        w[n, 4:7] = parcels[2:5, at]
        w[n, 7:8] = (cell[:, at] % 128).astype(F32)
        return carry

    lax.fori_loop(0, PAR_DEV // 128, columns, 0, unroll=2)
    w[PAR_DEV // 128] = jnp.zeros((8, 128), F32)

    shape = (N_SLAB * N_CROSS, 128)
    number = iota(0, shape)
    lane = iota(1, shape)
    live = count[0]

    def scan(n, carry):
        first, length = carry
        owner = box[:, pl.ds(pl.multiple_of(n * 128, 128), 128)] // 4
        here = owner == number
        position = lane + n * 128
        first = jnp.where(here, jnp.minimum(first, position), first)
        length = length + jnp.where(here & (position < live), 1, 0)
        return first, length

    first, length = lax.fori_loop(
        0,
        PAR_DEV // 128,
        scan,
        (jnp.full(shape, PAR_DEV - 1, jnp.int32), jnp.zeros(shape, jnp.int32)),
    )
    first = jnp.min(first, axis=1, keepdims=True)
    length = jnp.sum(length, axis=1, keepdims=True)
    spans_v[...] = jnp.where(lane == 0, first, length)
    copy = pltpu.make_async_copy(spans_v, spans_s, sem)
    copy.start()
    copy.wait()

    lane = iota(1)
    row = iota(0)

    def body(o, carry):
        start = spans_s[o, 0] & (PAR_DEV - 1)
        tile = lax.div(start, 128)
        first, second = w[tile], w[tile + 1]
        offset = jnp.full((8, 128), start, jnp.int32)
        ahead = pltpu.roll(jnp.where(lane < 64, second, first), 64, 1)
        window = jnp.where((offset & 64) != 0, ahead, first)
        for bit in (32, 16, 8, 4, 2, 1):
            window = jnp.where((offset & bit) != 0, pltpu.roll(window, 128 - bit, 1), window)
        window = jnp.where((row == 0) & (lane >= spans_s[o, 1]), 0.0, window)
        low = window[0:4]
        high = pltpu.roll(window, 64, 1)[4:8]
        out[o % N_CROSS, o // N_CROSS] = jnp.where(lane[0:4] < 64, low, high)
        return carry

    lax.fori_loop(0, N_SLAB * N_CROSS, body, 0, unroll=8)


def step_kernel(
    s_ref, v_ref, h_ref, d_ref, tg_ref, mass_ref, ps_ref, box_ref, cell_ref, count_ref,
    new_ref, tend_ref,
    *scratch,
):
    arrays = (s_ref, v_ref, h_ref)
    bufs = scratch[0:4]
    outs = scratch[4:8]
    placed = scratch[8:12]
    (xl, xh, zl, zh, z0, z15) = scratch[12:18]
    (sb, r1, r2) = scratch[18:21]
    (tgv, tgb, inv_v, inv_s, w, spans_v, spans_s) = scratch[21:28]
    (gx, hx, gy, hy, gz, hz, gzp, hzp, vals, tabs) = scratch[28:38]
    (tsem, p1, p2, hsem, psem, lsem) = scratch[38:44]

    me_s = lax.axis_index("slab")
    me_c = lax.axis_index("cross")

    def cross(d):
        return lax.rem(me_c + d, N_CROSS)

    def slab(d):
        return lax.rem(me_s + d, N_SLAB)

    barrier = pltpu.get_barrier_semaphore()

    def greet_c(d, carry):
        pl.semaphore_signal(barrier, inc=1, device_id=(me_s, cross(d)), device_id_type=MESH)
        return carry

    def greet_s(d, carry):
        pl.semaphore_signal(barrier, inc=1, device_id=(slab(d), me_c), device_id_type=MESH)
        return carry

    lax.fori_loop(1, N_CROSS, greet_c, 0)
    lax.fori_loop(1, N_SLAB, greet_s, 0)
    pl.semaphore_wait(barrier, N_CROSS - 1 + N_SLAB - 1)

    def remote(src, dst, sems, peer):
        return pltpu.make_async_remote_copy(
            src_ref=src,
            dst_ref=dst,
            send_sem=sems.at[0],
            recv_sem=sems.at[1],
            device_id=peer,
            device_id_type=MESH,
        )

    def drain(ref, sem):
        pltpu.make_async_copy(ref, ref, sem).wait()

    mine = jnp.zeros((8, 128), jnp.int32)
    for k in range(4):
        mine = mine + jnp.where(iota(1) == 4 * me_c + k, tg_ref[0, k], 0)
    tgv[...] = mine
    tgb[me_c] = mine

    def send_targets(d, carry):
        remote(tgv, tgb.at[me_c], tsem, (me_s, cross(d))).start()
        return carry

    lax.fori_loop(1, N_CROSS, send_targets, 0)

    def parts(g):
        at = 0
        for which, first, count in GROUPS[g]:
            yield arrays[which], first, count, at
            at += count

    def phase1(g):
        sems = p1.at[g]

        def body(d, carry):
            m = cross(d)
            for src, first, count, at in parts(g):
                remote(
                    src.at[pl.ds(first, count), m],
                    bufs[g].at[me_c, pl.ds(at, count)],
                    sems,
                    (me_s, m),
                ).start()
            return carry

        lax.fori_loop(1, N_CROSS, body, 0)
        for src, first, count, at in parts(g):
            pltpu.make_async_copy(
                src.at[pl.ds(first, count), me_c], bufs[g].at[me_c, pl.ds(at, count)], lsem.at[g]
            ).start()

    def phase2(g):
        width = WIDTHS[g]
        sems = p1.at[g]
        drain(bufs[g].at[pl.ds(0, N_CROSS - 1)], sems.at[1])
        drain(bufs[g].at[0], lsem.at[g])

        def fill(t):
            for q in range(4):
                code = inv_s[t * 4 + q, 0] & 63
                outs[g][t, :, q : q + 5 : 4, :] = bufs[g][
                    lax.div(code, 4), :, pl.ds(lax.rem(code, 4), 2, stride=4), :
                ]

        def body(d, carry):
            t = cross(d)
            fill(t)
            remote(outs[g].at[t], placed[g].at[me_c], p2.at[g], (me_s, t)).start()
            return carry

        lax.fori_loop(1, N_CROSS, body, 0)
        fill(me_c)
        pltpu.make_async_copy(outs[g].at[me_c], placed[g].at[me_c], lsem.at[g]).start()

    def landed(g):
        drain(placed[g].at[pl.ds(0, N_CROSS - 1)], p2.at[g, 1])
        drain(placed[g].at[0], lsem.at[g])

    def sent(g):
        drain(bufs[g].at[pl.ds(0, N_CROSS - 1)], p1.at[g, 0])
        drain(outs[g].at[pl.ds(0, N_CROSS - 1)], p2.at[g, 0])

    phase1(0)
    phase1(1)

    pack(mass_ref, ps_ref, box_ref, cell_ref, count_ref, w, spans_v, spans_s, lsem.at[4], sb)

    def parcels1(d, carry):
        c = cross(d)
        remote(sb.at[c], r1.at[me_c], psem.at[0], (me_s, c)).start()
        return carry

    lax.fori_loop(1, N_CROSS, parcels1, 0)

    drain(tgb.at[pl.ds(0, N_CROSS - 1)], tsem.at[1])
    flat = tgb[0]
    for s in range(1, N_CROSS):
        flat = flat + tgb[s]
    for tile in range(8):
        hit = flat == iota(0) + 8 * tile
        code = jnp.sum(jnp.where(hit & (iota(1) < 64), iota(1), 0), axis=1, keepdims=True)
        inv_v[8 * tile : 8 * tile + 8, :] = jnp.broadcast_to(code, (8, 128))
    to_scalar = pltpu.make_async_copy(inv_v, inv_s, lsem.at[4])
    to_scalar.start()
    to_scalar.wait()

    phase2(0)
    own = pltpu.make_async_copy(sb.at[me_c], r1.at[me_c], lsem.at[4])
    own.start()
    phase1(2)
    phase2(1)
    phase1(3)

    own.wait()
    drain(r1.at[pl.ds(0, N_CROSS - 1)], psem.at[0, 1])

    def parcels2(d, carry):
        a = slab(d)
        remote(r1.at[:, a], r2.at[me_s], psem.at[1], (a, me_c)).start()
        return carry

    lax.fori_loop(1, N_SLAB, parcels2, 0)
    own = pltpu.make_async_copy(r1.at[:, me_s], r2.at[me_s], lsem.at[4])
    own.start()

    landed(0)
    landed(1)
    x_lo = (me_s, cross(N_CROSS - 1))
    x_hi = (me_s, cross(1))
    halo = []
    for g in range(2):
        at, rows = pl.ds(sum(HALO[:g]), HALO[g]), pl.ds(0, HALO[g])
        halo.append(remote(placed[g].at[0, rows], xh.at[at], hsem.at[g], x_lo))
        halo.append(remote(placed[g].at[BE - 1, rows], xl.at[at], hsem.at[2 + g], x_hi))
    for copy in halo:
        copy.start()
    pack_z(placed, z0, z15)
    z_lo = (slab(N_SLAB - 1), me_c)
    z_hi = (slab(1), me_c)
    for copy in (remote(z0, zh, hsem.at[4], z_lo), remote(z15, zl, hsem.at[5], z_hi)):
        copy.start()
        halo.append(copy)

    phase2(2)
    for copy in halo:
        copy.wait()
    transport(
        d_ref, placed[0], placed[1], xl, xh, zl, zh, z0, z15, tend_ref,
        gx, hx, gy, hy, gz, hz, gzp, hzp,
    )
    phase2(3)
    advance(placed[0], 3, placed[1], 12, tend_ref, new_ref, 0, 1)
    advance(placed[1], 11, placed[1], 13, tend_ref, new_ref, FIELDS - 1, 1)
    own.wait()
    drain(r2.at[pl.ds(0, N_SLAB - 1)], psem.at[1, 1])
    deposit(placed[0], r2, new_ref, vals, tabs)
    landed(2)
    advance(placed[0], 4, placed[2], 0, tend_ref, new_ref, 1, 9)
    advance(placed[1], 0, placed[2], 9, tend_ref, new_ref, 10, 1)
    landed(3)
    advance(placed[1], 1, placed[3], 0, tend_ref, new_ref, 11, 10)

    drain(tgb.at[pl.ds(0, N_CROSS - 1)], tsem.at[0])
    drain(r1.at[pl.ds(0, N_CROSS - 1)], psem.at[0, 0])
    drain(r2.at[pl.ds(0, N_SLAB - 1)], psem.at[1, 0])
    for g in range(4):
        sent(g)


def pack_z(placed, z0, z15):
    lane16 = iota(1) // 16
    upper = iota(0) >= 4

    for g in range(2):
        first = sum(HALO[:g])

        def body(f, carry):
            low = [None, None]
            high = [None, None]
            for ih in range(2):
                for il in range(8):
                    x = placed[g][ih * 8 + il, f]
                    a = lane_roll(x, 16 * il)
                    b = lane_roll(x, 16 * il + 16)
                    if il == 0:
                        low[ih], high[ih] = a, b
                    else:
                        low[ih] = jnp.where(lane16 == il, a, low[ih])
                        high[ih] = jnp.where(lane16 == il, b, high[ih])
            z0[first + f] = jnp.where(upper, sub_roll(low[1], 4), low[0])
            z15[first + f] = jnp.where(upper, high[1], sub_roll(high[0], 4))
            return carry

        lax.fori_loop(0, HALO[g], body, 0)


def step(state, velocity, history, diffusion, targets, mass, parcels, box, cell, count):
    vm = pl.BlockSpec(memory_space=pltpu.VMEM)
    sm = pl.BlockSpec(memory_space=pltpu.SMEM)
    hbm = pl.BlockSpec(memory_space=pl.ANY)
    group = [(N_CROSS, w, 8, 128) for w in WIDTHS]
    devices = N_SLAB * N_CROSS
    out = jax.ShapeDtypeStruct((FIELDS, BE, 8, 128), F32)
    return pl.pallas_call(
        step_kernel,
        out_shape=[out, out],
        in_specs=[hbm, hbm, hbm, sm, sm, vm, vm, vm, vm, sm],
        out_specs=[vm, vm],
        scratch_shapes=[pltpu.VMEM(s, F32) for s in group * 3]
        + [pltpu.VMEM((sum(HALO), 8, 128), F32)] * 6
        + [pltpu.VMEM((N_CROSS, N_SLAB, 4, 128), F32)] * 2
        + [pltpu.VMEM((N_SLAB, N_CROSS, 4, 128), F32)]
        + [
            pltpu.VMEM((8, 128), jnp.int32),
            pltpu.VMEM((N_CROSS, 8, 128), jnp.int32),
            pltpu.VMEM((64, 128), jnp.int32),
            pltpu.SMEM((64, 128), jnp.int32),
            pltpu.VMEM((PAR_DEV // 128 + 1, 8, 128), F32),
            pltpu.VMEM((devices, 128), jnp.int32),
            pltpu.SMEM((devices, 128), jnp.int32),
        ]
        + [pltpu.VMEM((BE + 1, 8, 128), F32)] * 2
        + [pltpu.VMEM((BE, 8, 128), F32)] * 4
        + [pltpu.VMEM((2, 8, 128), F32)] * 2
        + [pltpu.VMEM((8, devices * CAP), F32), pltpu.VMEM((640, 256), BF16)]
        + [
            pltpu.SemaphoreType.DMA((2,)),
            pltpu.SemaphoreType.DMA((4, 2)),
            pltpu.SemaphoreType.DMA((4, 2)),
            pltpu.SemaphoreType.DMA((6, 2)),
            pltpu.SemaphoreType.DMA((2, 2)),
            pltpu.SemaphoreType.DMA((5,)),
        ],
        compiler_params=pltpu.CompilerParams(
            collective_id=0, has_side_effects=True, vmem_limit_bytes=VMEM_LIMIT
        ),
    )(state, velocity, history, diffusion, targets, mass, parcels, box, cell, count)


def spread_of(e):
    return 1.0 + 0.5 * jnp.tanh(e)


def transport(
    d_ref, p0, p1, xl, xh, zl, zh, z0, z15, tend_ref, gx, hx, gy, hy, gz, hz, gzp, hzp
):
    me_c = lax.axis_index("cross")
    lane = iota(1)
    row = iota(0)
    kl7 = lane >= 112
    kl0 = lane < 16
    top = kl7 & (row >= 4)
    bottom = kl0 & (row < 4)
    j15 = lane % 16 == 15
    j0 = lane % 16 == 0
    wall_y = j15 & (row % 4 == 3)

    def up_z(q):
        return lane_roll(jnp.where(kl0, sub_roll(q, 4), q), -16)

    def down_z(q):
        return lane_roll(jnp.where(kl7, sub_roll(q, 4), q), 16)

    def up_y(q):
        return jnp.where(j15, sub_roll(lane_roll(q, 15), -1), lane_roll(q, -1))

    def down_y(q):
        return jnp.where(j0, sub_roll(lane_roll(q, -15), 1), lane_roll(q, 1))

    def put_top(packed, i):
        ih, il = divmod(i, 8)
        return lane_roll(packed[1 - ih], 112 - 16 * il)

    def put_bottom(packed, i):
        ih, il = divmod(i, 8)
        return lane_roll(packed[ih], -16 * il)

    E = HALO[1] - 1
    EH = HALO[0] + HALO[1] - 1
    first_wall = jnp.where(me_c == 0, 0.0, 1.0)
    last_wall = jnp.where(me_c == N_CROSS - 1, 0.0, 1.0)
    before_g = spread_of(xl[EH])
    before_u = xl[0]
    for i in range(BE + 1):
        if i < BE:
            now_g, now_u = spread_of(p1[i, E]), p0[i, 0]
        else:
            now_g, now_u = spread_of(xh[EH]), xh[0]
        g, h = 0.5 * (before_g + now_g), 0.25 * (before_u + now_u)
        if i == 0:
            g, h = g * first_wall, h * first_wall
        if i == BE:
            g, h = g * last_wall, h * last_wall
        gx[i], hx[i] = g, h
        before_g, before_u = now_g, now_u
        if i < BE:
            uy, uz = p0[i, 1], p0[i, 2]
            gy[i] = jnp.where(wall_y, 0.0, 0.5 * (now_g + up_y(now_g)))
            hy[i] = jnp.where(wall_y, 0.0, 0.25 * (uy + up_y(uy)))
            gz[i] = 0.5 * (now_g + up_z(now_g))
            hz[i] = 0.25 * (uz + up_z(uz))
    gzp[0] = 0.5 * (spread_of(zl[EH]) + spread_of(z0[EH]))
    gzp[1] = 0.5 * (spread_of(z15[EH]) + spread_of(zh[EH]))
    hzp[0] = 0.25 * (zl[2] + z0[2])
    hzp[1] = 0.25 * (z15[2] + zh[2])

    def flux(d, g, h, low, high):
        return (d * g) * (high - low) - h * (high + low)

    def sweep(q_ref, q_at, x_at, out_at, count):
        def body(n, carry):
            f = out_at + n
            d = d_ref[f]
            xf = x_at + n
            qf = q_at + n
            edge0 = flux(d, gzp[0], hzp[0], zl[xf], z0[xf])
            edge15 = flux(d, gzp[1], hzp[1], z15[xf], zh[xf])
            edge0 = (edge0, sub_roll(edge0, 4))
            edge15 = (edge15, sub_roll(edge15, 4))
            q = q_ref[0, qf]
            fx = flux(d, gx[0], hx[0], xl[xf], q)
            for i in range(BE):
                ahead = q_ref[i + 1, qf] if i < BE - 1 else xh[xf]
                fx_up = flux(d, gx[i + 1], hx[i + 1], q, ahead)
                total = fx_up - fx
                fz = flux(d, gz[i], hz[i], q, up_z(q))
                fz = jnp.where(top, put_top(edge15, i), fz)
                fz_low = jnp.where(bottom, put_bottom(edge0, i), down_z(fz))
                total = total + fz - fz_low
                fy = flux(d, gy[i], hy[i], q, up_y(q))
                total = total + fy - down_y(fy)
                tend_ref[f, i] = total
                fx = fx_up
                q = ahead
            return carry

        lax.fori_loop(0, count, body, 0)

    sweep(p0, 3, 3, 0, 10)
    sweep(p1, 0, 13, 10, 12)


def advance(q_ref, q_at, h_ref, h_at, tend_ref, new_ref, f_at, count):
    def body(n, carry):
        new_ref[f_at + n] = q_ref[:, q_at + n] + TIME_STEP * (
            1.5 * tend_ref[f_at + n] - 0.5 * h_ref[:, h_at + n]
        )
        return carry

    lax.fori_loop(0, count, body, 0)


def deposit(p0, r2, new_ref, vals, tabs):
    tables = [new_ref[0], new_ref[FIELDS - 1]] + [p0[:, d] for d in range(3)]
    for n, table in enumerate(tables):
        table = table.reshape(128, 128)
        first = table.astype(BF16)
        tabs[128 * n : 128 * n + 128, 0:128] = first
        tabs[128 * n : 128 * n + 128, 128:256] = (table - first.astype(F32)).astype(BF16)

    half = iota(1, (4, 128)) < 64

    def unpack(n, carry):
        a, b = r2[n // 8, 2 * (n % 8)], r2[n // 8, 2 * (n % 8) + 1]
        at = pl.ds(pl.multiple_of(n * 128, 128), 128)
        vals[0:4, at] = jnp.where(half, a, pltpu.roll(b, 64, 1))
        vals[4:8, at] = jnp.where(half, pltpu.roll(a, 64, 1), b)
        return carry

    lax.fori_loop(0, 64, unpack, 0, unroll=4)

    number = lax.broadcasted_iota(jnp.int32, (128, CHUNK), 0).astype(F32)

    def add_chunk(n, acc):
        v = vals[:, pl.ds(pl.multiple_of(n * CHUNK, CHUNK), CHUNK)]
        at_row = number == v[3:4]
        at_lane = jnp.where(number == v[7:8], 1.0, 0.0).astype(BF16)
        picked = jnp.dot(
            tabs[...], jnp.concatenate([at_lane, at_lane], axis=0), preferred_element_type=F32
        )

        def value(m):
            return jnp.sum(
                jnp.where(at_row, picked[128 * m : 128 * m + 128], 0.0), axis=0, keepdims=True
            )

        slip = (value(2) - v[4:5]) ** 2 + (value(3) - v[5:6]) ** 2 + (value(4) - v[6:7]) ** 2
        coef = v[0:1] * jnp.sqrt(1.0 + slip)
        rate = coef * (v[1:2] - value(0))
        heat = coef * (v[2:3] - value(1)) - LATENT * rate
        rows = []
        for x in (rate, heat):
            first = x.astype(BF16).astype(F32)
            rows.append(jnp.where(at_row, first, 0.0).astype(BF16))
            rows.append(jnp.where(at_row, x - first, 0.0).astype(BF16))
        return acc + lax.dot_general(
            jnp.concatenate(rows, axis=0),
            at_lane,
            (((1,), (1,)), ((), ())),
            preferred_element_type=F32,
        )

    acc = lax.fori_loop(
        0, N_SLAB * N_CROSS * CAP // CHUNK, add_chunk, jnp.zeros((512, 128), F32)
    )
    fuel = (acc[0:128] + acc[128:256]).reshape(BE, 8, 128)
    heat = (acc[256:384] + acc[384:512]).reshape(BE, 8, 128)
    new_ref[0] = new_ref[0] + DEPOSIT * fuel
    new_ref[FIELDS - 1] = new_ref[FIELDS - 1] + DEPOSIT * heat


def to_tiles(array):
    fields = array.shape[0]
    return (
        array.reshape(fields, 4, 32, 128).transpose(0, 2, 1, 3).reshape(fields, BE, 8, 128)
    )


def from_tiles(array):
    fields = array.shape[0]
    return array.reshape(fields, 32, 4, 128).transpose(0, 2, 1, 3).reshape(fields, 4, 4096)


def per_device(
    state,
    velocity,
    history,
    diffusion,
    box_target,
    parcel_mass,
    parcel_state,
    parcel_box,
    parcel_cell,
    parcel_count,
):
    new_state, tendency = step(
        to_tiles(state),
        to_tiles(velocity),
        to_tiles(history),
        diffusion,
        box_target,
        parcel_mass[None],
        parcel_state,
        parcel_box[None],
        parcel_cell[None],
        parcel_count,
    )
    return from_tiles(new_state), from_tiles(tendency)


def solution(mesh):
    return jax.shard_map(
        per_device,
        mesh=mesh,
        in_specs=(
            P(None, ("slab", "cross"), None),
            P(None, ("slab", "cross"), None),
            P(None, ("slab", "cross"), None),
            P(),
            P("slab", "cross"),
            P(("slab", "cross")),
            P(None, ("slab", "cross")),
            P(("slab", "cross")),
            P(("slab", "cross")),
            P(("slab", "cross")),
        ),
        out_specs=(P(None, ("slab", "cross"), None), P(None, ("slab", "cross"), None)),
        check_vma=False,
    )
```

```python
import jax
import jax.numpy as jnp
from jax import lax
from jax.experimental import pallas as pl
from jax.experimental.pallas import tpu as pltpu
from jax.sharding import PartitionSpec as P

MESH = pl.DeviceIdType.MESH
F32 = jnp.float32
BF16 = jnp.bfloat16

BE = 16
PAR_DEV = 4096
CAP = 64
FIELDS = 22
N_SLAB = 8
N_CROSS = 16
CHUNK = 512
VMEM_LIMIT = 60 * 2**20

TIME_STEP = 0.2
LATENT = 0.5
DEPOSIT = 0.25

GROUPS = (
    ((1, 0, 3), (0, 0, 10)),
    ((0, 10, 12), (2, 0, 1), (2, 21, 1)),
    ((2, 1, 10),),
    ((2, 11, 10),),
)
WIDTHS = (13, 14, 10, 10)
HALO = (13, 12)


def iota(dim, shape=(8, 128)):
    return lax.broadcasted_iota(jnp.int32, shape, dim)


def lane_roll(x, shift):
    shift = shift % 128
    return x if shift == 0 else pltpu.roll(x, shift, x.ndim - 1)


def sub_roll(x, shift):
    shift = shift % 8
    return x if shift == 0 else pltpu.roll(x, shift, x.ndim - 2)


def pack(mass, parcels, box, cell, count, w, spans_v, spans_s, sem, out):
    def columns(n, carry):
        at = pl.ds(pl.multiple_of(n * 128, 128), 128)
        w[n, 0:1] = mass[:, at]
        w[n, 1:3] = parcels[0:2, at]
        w[n, 3:4] = ((cell[:, at] // 128) * 4 + box[:, at] % 4).astype(F32)
        w[n, 4:7] = parcels[2:5, at]
        w[n, 7:8] = (cell[:, at] % 128).astype(F32)
        return carry

    lax.fori_loop(0, PAR_DEV // 128, columns, 0, unroll=2)
    w[PAR_DEV // 128] = jnp.zeros((8, 128), F32)

    shape = (N_SLAB * N_CROSS, 128)
    number = iota(0, shape)
    lane = iota(1, shape)
    live = count[0]

    def scan(n, carry):
        first, length = carry
        owner = box[:, pl.ds(pl.multiple_of(n * 128, 128), 128)] // 4
        here = owner == number
        position = lane + n * 128
        first = jnp.where(here, jnp.minimum(first, position), first)
        length = length + jnp.where(here & (position < live), 1, 0)
        return first, length

    first, length = lax.fori_loop(
        0,
        PAR_DEV // 128,
        scan,
        (jnp.full(shape, PAR_DEV - 1, jnp.int32), jnp.zeros(shape, jnp.int32)),
    )
    first = jnp.min(first, axis=1, keepdims=True)
    length = jnp.sum(length, axis=1, keepdims=True)
    spans_v[...] = jnp.where(lane == 0, first, length)
    copy = pltpu.make_async_copy(spans_v, spans_s, sem)
    copy.start()
    copy.wait()

    lane = iota(1)
    row = iota(0)

    def body(o, carry):
        start = spans_s[o, 0] & (PAR_DEV - 1)
        tile = lax.div(start, 128)
        first, second = w[tile], w[tile + 1]
        offset = jnp.full((8, 128), start, jnp.int32)
        ahead = pltpu.roll(jnp.where(lane < 64, second, first), 64, 1)
        window = jnp.where((offset & 64) != 0, ahead, first)
        for bit in (32, 16, 8, 4, 2, 1):
            window = jnp.where((offset & bit) != 0, pltpu.roll(window, 128 - bit, 1), window)
        window = jnp.where((row == 0) & (lane >= spans_s[o, 1]), 0.0, window)
        low = window[0:4]
        high = pltpu.roll(window, 64, 1)[4:8]
        out[o % N_CROSS, o // N_CROSS] = jnp.where(lane[0:4] < 64, low, high)
        return carry

    lax.fori_loop(0, N_SLAB * N_CROSS, body, 0, unroll=8)


def step_kernel(
    s_ref, v_ref, h_ref, d_ref, tg_ref, mass_ref, ps_ref, box_ref, cell_ref, count_ref,
    new_ref, tend_ref,
    *scratch,
):
    arrays = (s_ref, v_ref, h_ref)
    bufs = scratch[0:4]
    outs = scratch[4:8]
    placed = scratch[8:12]
    (xl, xh, zl, zh, z0, z15) = scratch[12:18]
    (sb, r1, r2) = scratch[18:21]
    (tgv, tgb, inv_v, inv_s, w, spans_v, spans_s) = scratch[21:28]
    (gx, hx, gy, hy, gz, hz, gzp, hzp, vals, tabs) = scratch[28:38]
    (tsem, p1, p2, hsem, psem, lsem) = scratch[38:44]

    me_s = lax.axis_index("slab")
    me_c = lax.axis_index("cross")

    me_x, me_z = lax.div(me_c, 4), lax.rem(me_c, 4)

    def cross(d):
        return lax.rem(me_x + lax.div(d, 4), 4) * 4 + lax.rem(me_z + lax.rem(d, 4), 4)

    def slab(d):
        return lax.rem(me_s + d, N_SLAB)

    barrier = pltpu.get_barrier_semaphore()

    def greet_c(d, carry):
        pl.semaphore_signal(barrier, inc=1, device_id=(me_s, cross(d)), device_id_type=MESH)
        return carry

    def greet_s(d, carry):
        pl.semaphore_signal(barrier, inc=1, device_id=(slab(d), me_c), device_id_type=MESH)
        return carry

    lax.fori_loop(1, N_CROSS, greet_c, 0)
    lax.fori_loop(1, N_SLAB, greet_s, 0)
    pl.semaphore_wait(barrier, N_CROSS - 1 + N_SLAB - 1)

    def remote(src, dst, sems, peer):
        return pltpu.make_async_remote_copy(
            src_ref=src,
            dst_ref=dst,
            send_sem=sems.at[0],
            recv_sem=sems.at[1],
            device_id=peer,
            device_id_type=MESH,
        )

    def drain(ref, sem):
        pltpu.make_async_copy(ref, ref, sem).wait()

    mine = jnp.zeros((8, 128), jnp.int32)
    for k in range(4):
        mine = mine + jnp.where(iota(1) == 4 * me_c + k, tg_ref[0, k], 0)
    tgv[...] = mine
    tgb[me_c] = mine

    def send_targets(d, carry):
        remote(tgv, tgb.at[me_c], tsem, (me_s, cross(d))).start()
        return carry

    lax.fori_loop(1, N_CROSS, send_targets, 0)

    def parts(g):
        at = 0
        for which, first, count in GROUPS[g]:
            yield arrays[which], first, count, at
            at += count

    def phase1(g):
        sems = p1.at[g]

        def body(d, carry):
            m = cross(d)
            for src, first, count, at in parts(g):
                remote(
                    src.at[pl.ds(first, count), m],
                    bufs[g].at[me_c, pl.ds(at, count)],
                    sems,
                    (me_s, m),
                ).start()
            return carry

        lax.fori_loop(1, N_CROSS, body, 0)
        for src, first, count, at in parts(g):
            pltpu.make_async_copy(
                src.at[pl.ds(first, count), me_c], bufs[g].at[me_c, pl.ds(at, count)], lsem.at[g]
            ).start()

    def phase2(g):
        width = WIDTHS[g]
        sems = p1.at[g]
        drain(bufs[g].at[pl.ds(0, N_CROSS - 1)], sems.at[1])
        drain(bufs[g].at[0], lsem.at[g])

        def fill(t):
            for q in range(4):
                code = inv_s[t * 4 + q, 0] & 63
                outs[g][t, :, q : q + 5 : 4, :] = bufs[g][
                    lax.div(code, 4), :, pl.ds(lax.rem(code, 4), 2, stride=4), :
                ]

        def body(d, carry):
            t = cross(d)
            fill(t)
            remote(outs[g].at[t], placed[g].at[me_c], p2.at[g], (me_s, t)).start()
            return carry

        lax.fori_loop(1, N_CROSS, body, 0)
        fill(me_c)
        pltpu.make_async_copy(outs[g].at[me_c], placed[g].at[me_c], lsem.at[g]).start()

    def landed(g):
        drain(placed[g].at[pl.ds(0, N_CROSS - 1)], p2.at[g, 1])
        drain(placed[g].at[0], lsem.at[g])

    def sent(g):
        drain(bufs[g].at[pl.ds(0, N_CROSS - 1)], p1.at[g, 0])
        drain(outs[g].at[pl.ds(0, N_CROSS - 1)], p2.at[g, 0])

    phase1(0)
    phase1(1)

    pack(mass_ref, ps_ref, box_ref, cell_ref, count_ref, w, spans_v, spans_s, lsem.at[4], sb)

    def parcels1(d, carry):
        c = cross(d)
        remote(sb.at[c], r1.at[me_c], psem.at[0], (me_s, c)).start()
        return carry

    lax.fori_loop(1, N_CROSS, parcels1, 0)

    drain(tgb.at[pl.ds(0, N_CROSS - 1)], tsem.at[1])
    flat = tgb[0]
    for s in range(1, N_CROSS):
        flat = flat + tgb[s]
    for tile in range(8):
        hit = flat == iota(0) + 8 * tile
        code = jnp.sum(jnp.where(hit & (iota(1) < 64), iota(1), 0), axis=1, keepdims=True)
        inv_v[8 * tile : 8 * tile + 8, :] = jnp.broadcast_to(code, (8, 128))
    to_scalar = pltpu.make_async_copy(inv_v, inv_s, lsem.at[4])
    to_scalar.start()
    to_scalar.wait()

    phase2(0)
    own = pltpu.make_async_copy(sb.at[me_c], r1.at[me_c], lsem.at[4])
    own.start()
    phase2(1)

    own.wait()
    drain(r1.at[pl.ds(0, N_CROSS - 1)], psem.at[0, 1])

    def parcels2(d, carry):
        a = slab(d)
        remote(r1.at[:, a], r2.at[me_s], psem.at[1], (a, me_c)).start()
        return carry

    lax.fori_loop(1, N_SLAB, parcels2, 0)
    own = pltpu.make_async_copy(r1.at[:, me_s], r2.at[me_s], lsem.at[4])
    own.start()

    landed(0)
    phase1(2)
    landed(1)
    x_lo = (me_s, lax.rem(me_c + N_CROSS - 1, N_CROSS))
    x_hi = (me_s, lax.rem(me_c + 1, N_CROSS))
    halo = []
    for g in range(2):
        at, rows = pl.ds(sum(HALO[:g]), HALO[g]), pl.ds(0, HALO[g])
        halo.append(remote(placed[g].at[0, rows], xh.at[at], hsem.at[g], x_lo))
        halo.append(remote(placed[g].at[BE - 1, rows], xl.at[at], hsem.at[2 + g], x_hi))
    for copy in halo:
        copy.start()
    pack_z(placed, z0, z15)
    z_lo = (slab(N_SLAB - 1), me_c)
    z_hi = (slab(1), me_c)
    for copy in (remote(z0, zh, hsem.at[4], z_lo), remote(z15, zl, hsem.at[5], z_hi)):
        copy.start()
        halo.append(copy)

    phase1(3)
    phase2(2)
    for copy in halo:
        copy.wait()
    transport(
        d_ref, placed[0], placed[1], xl, xh, zl, zh, z0, z15, tend_ref,
        gx, hx, gy, hy, gz, hz, gzp, hzp,
    )
    phase2(3)
    advance(placed[0], 3, placed[1], 12, tend_ref, new_ref, 0, 1)
    advance(placed[1], 11, placed[1], 13, tend_ref, new_ref, FIELDS - 1, 1)
    own.wait()
    drain(r2.at[pl.ds(0, N_SLAB - 1)], psem.at[1, 1])
    deposit(placed[0], r2, new_ref, vals, tabs)
    landed(2)
    advance(placed[0], 4, placed[2], 0, tend_ref, new_ref, 1, 9)
    advance(placed[1], 0, placed[2], 9, tend_ref, new_ref, 10, 1)
    landed(3)
    advance(placed[1], 1, placed[3], 0, tend_ref, new_ref, 11, 10)

    drain(tgb.at[pl.ds(0, N_CROSS - 1)], tsem.at[0])
    drain(r1.at[pl.ds(0, N_CROSS - 1)], psem.at[0, 0])
    drain(r2.at[pl.ds(0, N_SLAB - 1)], psem.at[1, 0])
    for g in range(4):
        sent(g)


def pack_z(placed, z0, z15):
    lane16 = iota(1) // 16
    upper = iota(0) >= 4

    for g in range(2):
        first = sum(HALO[:g])

        def body(f, carry):
            low = [None, None]
            high = [None, None]
            for ih in range(2):
                for il in range(8):
                    x = placed[g][ih * 8 + il, f]
                    a = lane_roll(x, 16 * il)
                    b = lane_roll(x, 16 * il + 16)
                    if il == 0:
                        low[ih], high[ih] = a, b
                    else:
                        low[ih] = jnp.where(lane16 == il, a, low[ih])
                        high[ih] = jnp.where(lane16 == il, b, high[ih])
            z0[first + f] = jnp.where(upper, sub_roll(low[1], 4), low[0])
            z15[first + f] = jnp.where(upper, high[1], sub_roll(high[0], 4))
            return carry

        lax.fori_loop(0, HALO[g], body, 0)


def step(state, velocity, history, diffusion, targets, mass, parcels, box, cell, count):
    vm = pl.BlockSpec(memory_space=pltpu.VMEM)
    sm = pl.BlockSpec(memory_space=pltpu.SMEM)
    hbm = pl.BlockSpec(memory_space=pl.ANY)
    group = [(N_CROSS, w, 8, 128) for w in WIDTHS]
    devices = N_SLAB * N_CROSS
    out = jax.ShapeDtypeStruct((FIELDS, BE, 8, 128), F32)
    return pl.pallas_call(
        step_kernel,
        out_shape=[out, out],
        in_specs=[hbm, hbm, hbm, sm, sm, vm, vm, vm, vm, sm],
        out_specs=[vm, vm],
        scratch_shapes=[pltpu.VMEM(s, F32) for s in group * 3]
        + [pltpu.VMEM((sum(HALO), 8, 128), F32)] * 6
        + [pltpu.VMEM((N_CROSS, N_SLAB, 4, 128), F32)] * 2
        + [pltpu.VMEM((N_SLAB, N_CROSS, 4, 128), F32)]
        + [
            pltpu.VMEM((8, 128), jnp.int32),
            pltpu.VMEM((N_CROSS, 8, 128), jnp.int32),
            pltpu.VMEM((64, 128), jnp.int32),
            pltpu.SMEM((64, 128), jnp.int32),
            pltpu.VMEM((PAR_DEV // 128 + 1, 8, 128), F32),
            pltpu.VMEM((devices, 128), jnp.int32),
            pltpu.SMEM((devices, 128), jnp.int32),
        ]
        + [pltpu.VMEM((BE + 1, 8, 128), F32)] * 2
        + [pltpu.VMEM((BE, 8, 128), F32)] * 4
        + [pltpu.VMEM((2, 8, 128), F32)] * 2
        + [pltpu.VMEM((8, devices * CAP), F32), pltpu.VMEM((640, 256), BF16)]
        + [
            pltpu.SemaphoreType.DMA((2,)),
            pltpu.SemaphoreType.DMA((4, 2)),
            pltpu.SemaphoreType.DMA((4, 2)),
            pltpu.SemaphoreType.DMA((6, 2)),
            pltpu.SemaphoreType.DMA((2, 2)),
            pltpu.SemaphoreType.DMA((5,)),
        ],
        compiler_params=pltpu.CompilerParams(
            collective_id=0, has_side_effects=True, vmem_limit_bytes=VMEM_LIMIT
        ),
    )(state, velocity, history, diffusion, targets, mass, parcels, box, cell, count)


def spread_of(e):
    return 1.0 + 0.5 * jnp.tanh(e)


def transport(
    d_ref, p0, p1, xl, xh, zl, zh, z0, z15, tend_ref, gx, hx, gy, hy, gz, hz, gzp, hzp
):
    me_c = lax.axis_index("cross")
    lane = iota(1)
    row = iota(0)
    kl7 = lane >= 112
    kl0 = lane < 16
    top = kl7 & (row >= 4)
    bottom = kl0 & (row < 4)
    j15 = lane % 16 == 15
    j0 = lane % 16 == 0
    wall_y = j15 & (row % 4 == 3)

    def up_z(q):
        return lane_roll(jnp.where(kl0, sub_roll(q, 4), q), -16)

    def down_z(q):
        return lane_roll(jnp.where(kl7, sub_roll(q, 4), q), 16)

    def up_y(q):
        return jnp.where(j15, sub_roll(lane_roll(q, 15), -1), lane_roll(q, -1))

    def down_y(q):
        return jnp.where(j0, sub_roll(lane_roll(q, -15), 1), lane_roll(q, 1))

    def put_top(packed, i):
        ih, il = divmod(i, 8)
        return lane_roll(packed[1 - ih], 112 - 16 * il)

    def put_bottom(packed, i):
        ih, il = divmod(i, 8)
        return lane_roll(packed[ih], -16 * il)

    E = HALO[1] - 1
    EH = HALO[0] + HALO[1] - 1
    first_wall = jnp.where(me_c == 0, 0.0, 1.0)
    last_wall = jnp.where(me_c == N_CROSS - 1, 0.0, 1.0)
    before_g = spread_of(xl[EH])
    before_u = xl[0]
    for i in range(BE + 1):
        if i < BE:
            now_g, now_u = spread_of(p1[i, E]), p0[i, 0]
        else:
            now_g, now_u = spread_of(xh[EH]), xh[0]
        g, h = 0.5 * (before_g + now_g), 0.25 * (before_u + now_u)
        if i == 0:
            g, h = g * first_wall, h * first_wall
        if i == BE:
            g, h = g * last_wall, h * last_wall
        gx[i], hx[i] = g, h
        before_g, before_u = now_g, now_u
        if i < BE:
            uy, uz = p0[i, 1], p0[i, 2]
            gy[i] = jnp.where(wall_y, 0.0, 0.5 * (now_g + up_y(now_g)))
            hy[i] = jnp.where(wall_y, 0.0, 0.25 * (uy + up_y(uy)))
            gz[i] = 0.5 * (now_g + up_z(now_g))
            hz[i] = 0.25 * (uz + up_z(uz))
    gzp[0] = 0.5 * (spread_of(zl[EH]) + spread_of(z0[EH]))
    gzp[1] = 0.5 * (spread_of(z15[EH]) + spread_of(zh[EH]))
    hzp[0] = 0.25 * (zl[2] + z0[2])
    hzp[1] = 0.25 * (z15[2] + zh[2])

    def flux(d, g, h, low, high):
        return (d * g) * (high - low) - h * (high + low)

    def sweep(q_ref, q_at, x_at, out_at, count):
        def body(n, carry):
            f = out_at + n
            d = d_ref[f]
            xf = x_at + n
            qf = q_at + n
            edge0 = flux(d, gzp[0], hzp[0], zl[xf], z0[xf])
            edge15 = flux(d, gzp[1], hzp[1], z15[xf], zh[xf])
            edge0 = (edge0, sub_roll(edge0, 4))
            edge15 = (edge15, sub_roll(edge15, 4))
            q = q_ref[0, qf]
            fx = flux(d, gx[0], hx[0], xl[xf], q)
            for i in range(BE):
                ahead = q_ref[i + 1, qf] if i < BE - 1 else xh[xf]
                fx_up = flux(d, gx[i + 1], hx[i + 1], q, ahead)
                total = fx_up - fx
                fz = flux(d, gz[i], hz[i], q, up_z(q))
                fz = jnp.where(top, put_top(edge15, i), fz)
                fz_low = jnp.where(bottom, put_bottom(edge0, i), down_z(fz))
                total = total + fz - fz_low
                fy = flux(d, gy[i], hy[i], q, up_y(q))
                total = total + fy - down_y(fy)
                tend_ref[f, i] = total
                fx = fx_up
                q = ahead
            return carry

        lax.fori_loop(0, count, body, 0)

    sweep(p0, 3, 3, 0, 10)
    sweep(p1, 0, 13, 10, 12)


def advance(q_ref, q_at, h_ref, h_at, tend_ref, new_ref, f_at, count):
    def body(n, carry):
        new_ref[f_at + n] = q_ref[:, q_at + n] + TIME_STEP * (
            1.5 * tend_ref[f_at + n] - 0.5 * h_ref[:, h_at + n]
        )
        return carry

    lax.fori_loop(0, count, body, 0)


def deposit(p0, r2, new_ref, vals, tabs):
    tables = [new_ref[0], new_ref[FIELDS - 1]] + [p0[:, d] for d in range(3)]
    for n, table in enumerate(tables):
        table = table.reshape(128, 128)
        first = table.astype(BF16)
        tabs[128 * n : 128 * n + 128, 0:128] = first
        tabs[128 * n : 128 * n + 128, 128:256] = (table - first.astype(F32)).astype(BF16)

    half = iota(1, (4, 128)) < 64

    def unpack(n, carry):
        a, b = r2[n // 8, 2 * (n % 8)], r2[n // 8, 2 * (n % 8) + 1]
        at = pl.ds(pl.multiple_of(n * 128, 128), 128)
        vals[0:4, at] = jnp.where(half, a, pltpu.roll(b, 64, 1))
        vals[4:8, at] = jnp.where(half, pltpu.roll(a, 64, 1), b)
        return carry

    lax.fori_loop(0, 64, unpack, 0, unroll=4)

    number = lax.broadcasted_iota(jnp.int32, (128, CHUNK), 0).astype(F32)

    def add_chunk(n, acc):
        v = vals[:, pl.ds(pl.multiple_of(n * CHUNK, CHUNK), CHUNK)]
        at_row = number == v[3:4]
        at_lane = jnp.where(number == v[7:8], 1.0, 0.0).astype(BF16)
        picked = jnp.dot(
            tabs[...], jnp.concatenate([at_lane, at_lane], axis=0), preferred_element_type=F32
        )

        def value(m):
            return jnp.sum(
                jnp.where(at_row, picked[128 * m : 128 * m + 128], 0.0), axis=0, keepdims=True
            )

        slip = (value(2) - v[4:5]) ** 2 + (value(3) - v[5:6]) ** 2 + (value(4) - v[6:7]) ** 2
        coef = v[0:1] * jnp.sqrt(1.0 + slip)
        rate = coef * (v[1:2] - value(0))
        heat = coef * (v[2:3] - value(1)) - LATENT * rate
        rows = []
        for x in (rate, heat):
            first = x.astype(BF16).astype(F32)
            rows.append(jnp.where(at_row, first, 0.0).astype(BF16))
            rows.append(jnp.where(at_row, x - first, 0.0).astype(BF16))
        return acc + lax.dot_general(
            jnp.concatenate(rows, axis=0),
            at_lane,
            (((1,), (1,)), ((), ())),
            preferred_element_type=F32,
        )

    acc = lax.fori_loop(
        0, N_SLAB * N_CROSS * CAP // CHUNK, add_chunk, jnp.zeros((512, 128), F32)
    )
    fuel = (acc[0:128] + acc[128:256]).reshape(BE, 8, 128)
    heat = (acc[256:384] + acc[384:512]).reshape(BE, 8, 128)
    new_ref[0] = new_ref[0] + DEPOSIT * fuel
    new_ref[FIELDS - 1] = new_ref[FIELDS - 1] + DEPOSIT * heat


def to_tiles(array):
    fields = array.shape[0]
    return (
        array.reshape(fields, 4, 32, 128).transpose(0, 2, 1, 3).reshape(fields, BE, 8, 128)
    )


def from_tiles(array):
    fields = array.shape[0]
    return array.reshape(fields, 32, 4, 128).transpose(0, 2, 1, 3).reshape(fields, 4, 4096)


def per_device(
    state,
    velocity,
    history,
    diffusion,
    box_target,
    parcel_mass,
    parcel_state,
    parcel_box,
    parcel_cell,
    parcel_count,
):
    new_state, tendency = step(
        to_tiles(state),
        to_tiles(velocity),
        to_tiles(history),
        diffusion,
        box_target,
        parcel_mass[None],
        parcel_state,
        parcel_box[None],
        parcel_cell[None],
        parcel_count,
    )
    return from_tiles(new_state), from_tiles(tendency)


def solution(mesh):
    return jax.shard_map(
        per_device,
        mesh=mesh,
        in_specs=(
            P(None, ("slab", "cross"), None),
            P(None, ("slab", "cross"), None),
            P(None, ("slab", "cross"), None),
            P(),
            P("slab", "cross"),
            P(("slab", "cross")),
            P(None, ("slab", "cross")),
            P(("slab", "cross")),
            P(("slab", "cross")),
            P(("slab", "cross")),
        ),
        out_specs=(P(None, ("slab", "cross"), None), P(None, ("slab", "cross"), None)),
        check_vma=False,
    )
```

```python
import jax
import jax.numpy as jnp
from jax import lax
from jax.experimental import pallas as pl
from jax.experimental.pallas import tpu as pltpu
from jax.sharding import PartitionSpec as P

MESH = pl.DeviceIdType.MESH
F32 = jnp.float32
BF16 = jnp.bfloat16

BE = 16
PAR_DEV = 4096
CAP = 64
FIELDS = 22
N_SLAB = 8
N_CROSS = 16
CHUNK = 512
VMEM_LIMIT = 60 * 2**20

TIME_STEP = 0.2
LATENT = 0.5
DEPOSIT = 0.25

GROUPS = (
    ((1, 0, 3), (0, 0, 4)),
    ((0, 4, 6),),
    ((0, 10, 6),),
    ((0, 16, 6), (2, 0, 1), (2, 21, 1)),
    ((2, 1, 5),),
    ((2, 6, 5),),
    ((2, 11, 5),),
    ((2, 16, 5),),
)
WIDTHS = tuple(sum(part[2] for part in group) for group in GROUPS)
N_GAS = 4
GAS = tuple(sum(part[2] for part in group if part[0] < 2) for group in GROUPS[:N_GAS])

SCHEDULE = (
    ("1", 0), ("1", 1), ("1", 2), ("1", 3),
    ("pack", 0), ("invert", 0),
    ("2", 0), ("2", 1), ("2", 2), ("2", 3), ("pass", 0),
    ("landed", 0), ("landed", 1), ("1", 4), ("landed", 2), ("landed", 3),
    ("halo", 0), ("1", 5), ("1", 6), ("1", 7), ("faces", 0), ("sweep", 0), ("sweep", 1), ("sweep", 2), ("sweep", 3), ("2", 4), ("2", 5), ("2", 6), ("2", 7),
    ("advance", 3), ("parcels", 0), ("chunks", 0), ("chunks", 1), ("chunks", 2), ("chunks", 3), ("deposit", 0),
    ("landed", 4), ("advance", 4), ("landed", 5), ("advance", 5), ("landed", 6), ("advance", 6), ("landed", 7), ("advance", 7),
)


def runs(which):
    found = []
    for g, group in enumerate(GROUPS):
        row = 0
        for source, first, count in group:
            if source == which:
                found.append((first, count, g, row))
            row += count
    return sorted(found)


def place_of(which, field):
    for first, count, g, row in runs(which):
        if first <= field < first + count:
            return g, row + field - first, first + count - field


def iota(dim, shape=(8, 128)):
    return lax.broadcasted_iota(jnp.int32, shape, dim)


def lane_roll(x, shift):
    shift = shift % 128
    return x if shift == 0 else pltpu.roll(x, shift, x.ndim - 1)


def sub_roll(x, shift):
    shift = shift % 8
    return x if shift == 0 else pltpu.roll(x, shift, x.ndim - 2)


def pack(mass, parcels, box, cell, count, w, spans_v, spans_s, sem, out):
    def columns(n, carry):
        at = pl.ds(pl.multiple_of(n * 128, 128), 128)
        w[n, 0:1] = mass[:, at]
        w[n, 1:3] = parcels[0:2, at]
        w[n, 3:4] = ((cell[:, at] // 128) * 4 + box[:, at] % 4).astype(F32)
        w[n, 4:7] = parcels[2:5, at]
        w[n, 7:8] = (cell[:, at] % 128).astype(F32)
        return carry

    lax.fori_loop(0, PAR_DEV // 128, columns, 0, unroll=2)
    w[PAR_DEV // 128] = jnp.zeros((8, 128), F32)

    shape = (N_SLAB * N_CROSS, 128)
    number = iota(0, shape)
    lane = iota(1, shape)
    live = count[0]

    def scan(n, carry):
        first, length = carry
        owner = box[:, pl.ds(pl.multiple_of(n * 128, 128), 128)] // 4
        here = owner == number
        position = lane + n * 128
        first = jnp.where(here, jnp.minimum(first, position), first)
        length = length + jnp.where(here & (position < live), 1, 0)
        return first, length

    first, length = lax.fori_loop(
        0,
        PAR_DEV // 128,
        scan,
        (jnp.full(shape, PAR_DEV - 1, jnp.int32), jnp.zeros(shape, jnp.int32)),
    )
    first = jnp.min(first, axis=1, keepdims=True)
    length = jnp.sum(length, axis=1, keepdims=True)
    spans_v[...] = jnp.where(lane == 0, first, length)
    copy = pltpu.make_async_copy(spans_v, spans_s, sem)
    copy.start()
    copy.wait()

    lane = iota(1)
    row = iota(0)

    def body(o, carry):
        start = spans_s[o, 0] & (PAR_DEV - 1)
        tile = lax.div(start, 128)
        first, second = w[tile], w[tile + 1]
        offset = jnp.full((8, 128), start, jnp.int32)
        ahead = pltpu.roll(jnp.where(lane < 64, second, first), 64, 1)
        window = jnp.where((offset & 64) != 0, ahead, first)
        for bit in (32, 16, 8, 4, 2, 1):
            window = jnp.where((offset & bit) != 0, pltpu.roll(window, 128 - bit, 1), window)
        window = jnp.where((row == 0) & (lane >= spans_s[o, 1]), 0.0, window)
        low = window[0:4]
        high = pltpu.roll(window, 64, 1)[4:8]
        out[o % N_CROSS, o // N_CROSS] = jnp.where(lane[0:4] < 64, low, high)
        return carry

    lax.fori_loop(0, N_SLAB * N_CROSS, body, 0, unroll=8)


def step_kernel(
    s_ref, v_ref, h_ref, d_ref, tg_ref, mass_ref, ps_ref, box_ref, cell_ref, count_ref,
    new_out, tend_out,
    *scratch,
):
    arrays = (s_ref, v_ref, h_ref)
    n = len(GROUPS)
    bufs, outs, placed = scratch[0:n], scratch[n : 2 * n], scratch[2 * n : 3 * n]
    scratch = scratch[3 * n :]
    (xl, xh, zl, zh, z0, z15) = scratch[0:6]
    (sb, r1, r2) = scratch[6:9]
    (tgv, tgb, inv_v, inv_s, w, spans_v, spans_s) = scratch[9:16]
    (gx, hx, gy, hy, gz, hz, gzp, hzp, vals, tabs) = scratch[16:26]
    (tsem, p1, p2, hsem, psem, lsem) = scratch[26:32]
    (new_ref, tend_ref, osem) = scratch[32:35]

    me_s = lax.axis_index("slab")
    me_c = lax.axis_index("cross")

    me_x, me_z = lax.div(me_c, 4), lax.rem(me_c, 4)

    def cross(d):
        return lax.rem(me_x + lax.div(d, 4), 4) * 4 + lax.rem(me_z + lax.rem(d, 4), 4)

    def slab(d):
        return lax.rem(me_s + d, N_SLAB)

    barrier = pltpu.get_barrier_semaphore()

    def greet_c(d, carry):
        pl.semaphore_signal(barrier, inc=1, device_id=(me_s, cross(d)), device_id_type=MESH)
        return carry

    def greet_s(d, carry):
        pl.semaphore_signal(barrier, inc=1, device_id=(slab(d), me_c), device_id_type=MESH)
        return carry

    lax.fori_loop(1, N_CROSS, greet_c, 0)
    lax.fori_loop(1, N_SLAB, greet_s, 0)
    pl.semaphore_wait(barrier, N_CROSS - 1 + N_SLAB - 1)

    def remote(src, dst, sems, peer):
        return pltpu.make_async_remote_copy(
            src_ref=src,
            dst_ref=dst,
            send_sem=sems.at[0],
            recv_sem=sems.at[1],
            device_id=peer,
            device_id_type=MESH,
        )

    def drain(ref, sem):
        pltpu.make_async_copy(ref, ref, sem).wait()

    mine = jnp.zeros((8, 128), jnp.int32)
    for k in range(4):
        mine = mine + jnp.where(iota(1) == 4 * me_c + k, tg_ref[0, k], 0)
    tgv[...] = mine
    tgb[me_c] = mine

    def send_targets(d, carry):
        remote(tgv, tgb.at[me_c], tsem, (me_s, cross(d))).start()
        return carry

    lax.fori_loop(1, N_CROSS, send_targets, 0)

    def parts(g):
        at = 0
        for which, first, count in GROUPS[g]:
            yield arrays[which], first, count, at
            at += count

    def phase1(g):
        sems = p1.at[g]

        def body(d, carry):
            m = cross(d)
            for src, first, count, at in parts(g):
                remote(
                    src.at[pl.ds(first, count), m],
                    bufs[g].at[me_c, pl.ds(at, count)],
                    sems,
                    (me_s, m),
                ).start()
            return carry

        lax.fori_loop(1, N_CROSS, body, 0)
        for src, first, count, at in parts(g):
            pltpu.make_async_copy(
                src.at[pl.ds(first, count), me_c], bufs[g].at[me_c, pl.ds(at, count)], lsem.at[g]
            ).start()

    def phase2(g):
        width = WIDTHS[g]
        sems = p1.at[g]
        drain(bufs[g].at[pl.ds(0, N_CROSS - 1)], sems.at[1])
        drain(bufs[g].at[0], lsem.at[g])

        def fill(t):
            for q in range(4):
                code = inv_s[t * 4 + q, 0] & 63
                outs[g][t, :, q : q + 5 : 4, :] = bufs[g][
                    lax.div(code, 4), :, pl.ds(lax.rem(code, 4), 2, stride=4), :
                ]

        def body(d, carry):
            t = cross(d)
            fill(t)
            remote(outs[g].at[t], placed[g].at[me_c], p2.at[g], (me_s, t)).start()
            return carry

        lax.fori_loop(1, N_CROSS, body, 0)
        fill(me_c)
        pltpu.make_async_copy(outs[g].at[me_c], placed[g].at[me_c], lsem.at[g]).start()

    def landed(g):
        drain(placed[g].at[pl.ds(0, N_CROSS - 1)], p2.at[g, 1])
        drain(placed[g].at[0], lsem.at[g])

    def sent(g):
        drain(bufs[g].at[pl.ds(0, N_CROSS - 1)], p1.at[g, 0])
        drain(outs[g].at[pl.ds(0, N_CROSS - 1)], p2.at[g, 0])

    def invert():
        drain(tgb.at[pl.ds(0, N_CROSS - 1)], tsem.at[1])
        flat = tgb[0]
        for s in range(1, N_CROSS):
            flat = flat + tgb[s]
        for tile in range(8):
            hit = flat == iota(0) + 8 * tile
            code = jnp.sum(jnp.where(hit & (iota(1) < 64), iota(1), 0), axis=1, keepdims=True)
            inv_v[8 * tile : 8 * tile + 8, :] = jnp.broadcast_to(code, (8, 128))
        to_scalar = pltpu.make_async_copy(inv_v, inv_s, lsem.at[n])
        to_scalar.start()
        to_scalar.wait()

    halo = []

    def send_halos():
        x_lo = (me_s, lax.rem(me_c + N_CROSS - 1, N_CROSS))
        x_hi = (me_s, lax.rem(me_c + 1, N_CROSS))
        for g in range(N_GAS):
            at = pl.ds(sum(GAS[:g]), GAS[g])
            rows = pl.ds(0, GAS[g])
            halo.append(remote(placed[g].at[0, rows], xh.at[at], hsem.at[2 * g], x_lo))
            halo.append(remote(placed[g].at[BE - 1, rows], xl.at[at], hsem.at[2 * g + 1], x_hi))
        for copy in halo:
            copy.start()
        pack_z(placed, z0, z15)
        z_lo = (slab(N_SLAB - 1), me_c)
        z_hi = (slab(1), me_c)
        for copy in (
            remote(z0, zh, hsem.at[2 * N_GAS], z_lo),
            remote(z15, zl, hsem.at[2 * N_GAS + 1], z_hi),
        ):
            copy.start()
            halo.append(copy)

    def parcels1(d, carry):
        c = cross(d)
        remote(sb.at[c], r1.at[me_c], psem.at[0], (me_s, c)).start()
        return carry

    def parcels2(d, carry):
        a = slab(d)
        remote(r1.at[:, a], r2.at[me_s], psem.at[1], (a, me_c)).start()
        return carry

    kept = {}

    def write(ref, out, sem, first, count):
        at = pl.ds(first, count)
        pltpu.make_async_copy(ref.at[at], out.at[at], sem).start()

    chunks = N_SLAB * N_CROSS * CAP // CHUNK
    for name, g in SCHEDULE:
        if name == "1":
            phase1(g)
        elif name == "2":
            phase2(g)
        elif name == "landed":
            landed(g)
        elif name == "pack":
            pack(mass_ref, ps_ref, box_ref, cell_ref, count_ref, w, spans_v, spans_s, lsem.at[n], sb)
            lax.fori_loop(1, N_CROSS, parcels1, 0)
            own = pltpu.make_async_copy(sb.at[me_c], r1.at[me_c], lsem.at[n])
            own.start()
            own.wait()
        elif name == "invert":
            invert()
        elif name == "pass":
            drain(r1.at[pl.ds(0, N_CROSS - 1)], psem.at[0, 1])
            lax.fori_loop(1, N_SLAB, parcels2, 0)
            own = pltpu.make_async_copy(r1.at[:, me_s], r2.at[me_s], lsem.at[n])
            own.start()
            own.wait()
        elif name == "halo":
            send_halos()
        elif name == "faces":
            for copy in halo:
                copy.wait()
            kept["sweep"] = faces(
                d_ref, placed, xl, xh, zl, zh, z0, z15, tend_ref,
                gx, hx, gy, hy, gz, hz, gzp, hzp,
            )
        elif name == "sweep":
            kept["sweep"](g)
            for first, count, group, _ in runs(0):
                if group == g:
                    write(tend_ref, tend_out, osem.at[0], first, count)
        elif name == "advance":
            advance(placed, g, tend_ref, new_ref)
            for first, count, group, _ in runs(2):
                if group == g and first not in (0, FIELDS - 1):
                    write(new_ref, new_out, osem.at[1], first, count)
        elif name == "parcels":
            drain(r2.at[pl.ds(0, N_SLAB - 1)], psem.at[1, 1])
            deposit_start(placed[0], r2, new_ref, vals, tabs)
            kept["acc"] = jnp.zeros((512, 128), F32)
        elif name == "chunks":
            low, high = chunks * g // 4, chunks * (g + 1) // 4
            kept["acc"] = deposit_chunks(low, high, kept["acc"], vals, tabs)
        elif name == "deposit":
            deposit_end(kept["acc"], new_ref)
            write(new_ref, new_out, osem.at[1], 0, 1)
            write(new_ref, new_out, osem.at[1], FIELDS - 1, 1)

    drain(tend_ref, osem.at[0])
    drain(new_ref, osem.at[1])
    drain(tgb.at[pl.ds(0, N_CROSS - 1)], tsem.at[0])
    drain(r1.at[pl.ds(0, N_CROSS - 1)], psem.at[0, 0])
    drain(r2.at[pl.ds(0, N_SLAB - 1)], psem.at[1, 0])
    for g in range(n):
        sent(g)


def pack_z(placed, z0, z15):
    lane16 = iota(1) // 16
    upper = iota(0) >= 4

    for g in range(N_GAS):
        first = sum(GAS[:g])

        def body(f, carry):
            low = [None, None]
            high = [None, None]
            for ih in range(2):
                for il in range(8):
                    x = placed[g][ih * 8 + il, f]
                    a = lane_roll(x, 16 * il)
                    b = lane_roll(x, 16 * il + 16)
                    if il == 0:
                        low[ih], high[ih] = a, b
                    else:
                        low[ih] = jnp.where(lane16 == il, a, low[ih])
                        high[ih] = jnp.where(lane16 == il, b, high[ih])
            z0[first + f] = jnp.where(upper, sub_roll(low[1], 4), low[0])
            z15[first + f] = jnp.where(upper, high[1], sub_roll(high[0], 4))
            return carry

        lax.fori_loop(0, GAS[g], body, 0)


def step(state, velocity, history, diffusion, targets, mass, parcels, box, cell, count):
    vm = pl.BlockSpec(memory_space=pltpu.VMEM)
    sm = pl.BlockSpec(memory_space=pltpu.SMEM)
    hbm = pl.BlockSpec(memory_space=pl.ANY)
    group = [(N_CROSS, w, 8, 128) for w in WIDTHS]
    devices = N_SLAB * N_CROSS
    out = jax.ShapeDtypeStruct((FIELDS, BE, 8, 128), F32)
    return pl.pallas_call(
        step_kernel,
        out_shape=[out, out],
        in_specs=[hbm, hbm, hbm, sm, sm, vm, vm, vm, vm, sm],
        out_specs=[hbm, hbm],
        scratch_shapes=[pltpu.VMEM(s, F32) for s in group * 3]
        + [pltpu.VMEM((sum(GAS), 8, 128), F32)] * 6
        + [pltpu.VMEM((N_CROSS, N_SLAB, 4, 128), F32)] * 2
        + [pltpu.VMEM((N_SLAB, N_CROSS, 4, 128), F32)]
        + [
            pltpu.VMEM((8, 128), jnp.int32),
            pltpu.VMEM((N_CROSS, 8, 128), jnp.int32),
            pltpu.VMEM((64, 128), jnp.int32),
            pltpu.SMEM((64, 128), jnp.int32),
            pltpu.VMEM((PAR_DEV // 128 + 1, 8, 128), F32),
            pltpu.VMEM((devices, 128), jnp.int32),
            pltpu.SMEM((devices, 128), jnp.int32),
        ]
        + [pltpu.VMEM((BE + 1, 8, 128), F32)] * 2
        + [pltpu.VMEM((BE, 8, 128), F32)] * 4
        + [pltpu.VMEM((2, 8, 128), F32)] * 2
        + [pltpu.VMEM((8, devices * CAP), F32), pltpu.VMEM((640, 256), BF16)]
        + [
            pltpu.SemaphoreType.DMA((2,)),
            pltpu.SemaphoreType.DMA((len(GROUPS), 2)),
            pltpu.SemaphoreType.DMA((len(GROUPS), 2)),
            pltpu.SemaphoreType.DMA((2 * N_GAS + 2, 2)),
            pltpu.SemaphoreType.DMA((2, 2)),
            pltpu.SemaphoreType.DMA((len(GROUPS) + 1,)),
            pltpu.VMEM((FIELDS, BE, 8, 128), F32),
            pltpu.VMEM((FIELDS, BE, 8, 128), F32),
            pltpu.SemaphoreType.DMA((2,)),
        ],
        compiler_params=pltpu.CompilerParams(
            collective_id=0, has_side_effects=True, vmem_limit_bytes=VMEM_LIMIT
        ),
    )(state, velocity, history, diffusion, targets, mass, parcels, box, cell, count)


def hand_over_kernel(a_ref, b_ref, a_out, b_out, a_held, b_held, sems):
    parts = 2
    steps = []
    for k, (src, held, dst) in enumerate(((a_ref, a_held, a_out), (b_ref, b_held, b_out))):
        for part in range(parts):
            at = pl.ds(part * (FIELDS // parts), FIELDS // parts)
            steps.append(
                (
                    pltpu.make_async_copy(src.at[at], held.at[at], sems.at[0, parts * k + part]),
                    pltpu.make_async_copy(held.at[at], dst.at[at], sems.at[1, parts * k + part]),
                )
            )
    for fetch, _ in steps:
        fetch.start()
    for fetch, store in steps:
        fetch.wait()
        store.start()
    for _, store in steps:
        store.wait()


def hand_over(a, b):
    hbm = pl.BlockSpec(memory_space=pl.ANY)
    out = jax.ShapeDtypeStruct((FIELDS, BE, 8, 128), F32)
    return pl.pallas_call(
        hand_over_kernel,
        out_shape=[out, out],
        in_specs=[hbm, hbm],
        out_specs=[hbm, hbm],
        scratch_shapes=[pltpu.VMEM((FIELDS, BE, 8, 128), F32)] * 2
        + [pltpu.SemaphoreType.DMA((2, 4))],
        compiler_params=pltpu.CompilerParams(vmem_limit_bytes=VMEM_LIMIT),
    )(a, b)


def spread_of(e):
    return 1.0 + 0.5 * jnp.tanh(e)


def faces(
    d_ref, placed, xl, xh, zl, zh, z0, z15, tend_ref, gx, hx, gy, hy, gz, hz, gzp, hzp
):
    me_c = lax.axis_index("cross")
    lane = iota(1)
    row = iota(0)
    kl7 = lane >= 112
    kl0 = lane < 16
    top = kl7 & (row >= 4)
    bottom = kl0 & (row < 4)
    j15 = lane % 16 == 15
    j0 = lane % 16 == 0
    wall_y = j15 & (row % 4 == 3)

    def up_z(q):
        return lane_roll(jnp.where(kl0, sub_roll(q, 4), q), -16)

    def down_z(q):
        return lane_roll(jnp.where(kl7, sub_roll(q, 4), q), 16)

    def up_y(q):
        return jnp.where(j15, sub_roll(lane_roll(q, 15), -1), lane_roll(q, -1))

    def down_y(q):
        return jnp.where(j0, sub_roll(lane_roll(q, -15), 1), lane_roll(q, 1))

    def put_top(packed, i):
        ih, il = divmod(i, 8)
        return lane_roll(packed[1 - ih], 112 - 16 * il)

    def put_bottom(packed, i):
        ih, il = divmod(i, 8)
        return lane_roll(packed[ih], -16 * il)

    p0 = placed[0]
    pe, E, _ = place_of(0, FIELDS - 1)
    EH = sum(GAS[:pe]) + E
    pe = placed[pe]
    first_wall = jnp.where(me_c == 0, 0.0, 1.0)
    last_wall = jnp.where(me_c == N_CROSS - 1, 0.0, 1.0)
    before_g = spread_of(xl[EH])
    before_u = xl[0]
    for i in range(BE + 1):
        if i < BE:
            now_g, now_u = spread_of(pe[i, E]), p0[i, 0]
        else:
            now_g, now_u = spread_of(xh[EH]), xh[0]
        g, h = 0.5 * (before_g + now_g), 0.25 * (before_u + now_u)
        if i == 0:
            g, h = g * first_wall, h * first_wall
        if i == BE:
            g, h = g * last_wall, h * last_wall
        gx[i], hx[i] = g, h
        before_g, before_u = now_g, now_u
        if i < BE:
            uy, uz = p0[i, 1], p0[i, 2]
            gy[i] = jnp.where(wall_y, 0.0, 0.5 * (now_g + up_y(now_g)))
            hy[i] = jnp.where(wall_y, 0.0, 0.25 * (uy + up_y(uy)))
            gz[i] = 0.5 * (now_g + up_z(now_g))
            hz[i] = 0.25 * (uz + up_z(uz))
    gzp[0] = 0.5 * (spread_of(zl[EH]) + spread_of(z0[EH]))
    gzp[1] = 0.5 * (spread_of(z15[EH]) + spread_of(zh[EH]))
    hzp[0] = 0.25 * (zl[2] + z0[2])
    hzp[1] = 0.25 * (z15[2] + zh[2])

    def flux(d, g, h, low, high):
        return (d * g) * (high - low) - h * (high + low)

    def sweep(q_ref, q_at, x_at, out_at, count):
        def body(n, carry):
            f = out_at + n
            d = d_ref[f]
            xf = x_at + n
            qf = q_at + n
            edge0 = flux(d, gzp[0], hzp[0], zl[xf], z0[xf])
            edge15 = flux(d, gzp[1], hzp[1], z15[xf], zh[xf])
            edge0 = (edge0, sub_roll(edge0, 4))
            edge15 = (edge15, sub_roll(edge15, 4))
            q = q_ref[0, qf]
            fx = flux(d, gx[0], hx[0], xl[xf], q)
            for i in range(BE):
                ahead = q_ref[i + 1, qf] if i < BE - 1 else xh[xf]
                fx_up = flux(d, gx[i + 1], hx[i + 1], q, ahead)
                total = fx_up - fx
                fz = flux(d, gz[i], hz[i], q, up_z(q))
                fz = jnp.where(top, put_top(edge15, i), fz)
                fz_low = jnp.where(bottom, put_bottom(edge0, i), down_z(fz))
                total = total + fz - fz_low
                fy = flux(d, gy[i], hy[i], q, up_y(q))
                total = total + fy - down_y(fy)
                tend_ref[f, i] = total
                fx = fx_up
                q = ahead
            return carry

        lax.fori_loop(0, count, body, 0)

    def sweep_group(g):
        for first, count, group, row in runs(0):
            if group == g:
                sweep(placed[g], row, sum(GAS[:g]) + row, first, count)

    return sweep_group


def advance(placed, g, tend_ref, new_ref):
    for first, count, group, h_row in runs(2):
        if group != g:
            continue
        f = first
        while f < first + count:
            q_group, q_row, left = place_of(0, f)
            many = min(left, first + count - f)
            advance_run(placed[q_group], q_row, placed[g], h_row + f - first, tend_ref, new_ref, f, many)
            f += many


def advance_run(q_ref, q_at, h_ref, h_at, tend_ref, new_ref, f_at, count):
    def body(m, carry):
        new_ref[f_at + m] = q_ref[:, q_at + m] + TIME_STEP * (
            1.5 * tend_ref[f_at + m] - 0.5 * h_ref[:, h_at + m]
        )
        return carry

    lax.fori_loop(0, count, body, 0)


def deposit_start(p0, r2, new_ref, vals, tabs):
    tables = [new_ref[0], new_ref[FIELDS - 1]] + [p0[:, d] for d in range(3)]
    for n, table in enumerate(tables):
        table = table.reshape(128, 128)
        first = table.astype(BF16)
        tabs[128 * n : 128 * n + 128, 0:128] = first
        tabs[128 * n : 128 * n + 128, 128:256] = (table - first.astype(F32)).astype(BF16)

    half = iota(1, (4, 128)) < 64

    def unpack(n, carry):
        a, b = r2[n // 8, 2 * (n % 8)], r2[n // 8, 2 * (n % 8) + 1]
        at = pl.ds(pl.multiple_of(n * 128, 128), 128)
        vals[0:4, at] = jnp.where(half, a, pltpu.roll(b, 64, 1))
        vals[4:8, at] = jnp.where(half, pltpu.roll(a, 64, 1), b)
        return carry

    lax.fori_loop(0, 64, unpack, 0, unroll=4)


def deposit_chunks(low, high, acc, vals, tabs):
    number = lax.broadcasted_iota(jnp.int32, (128, CHUNK), 0).astype(F32)

    def add_chunk(n, acc):
        v = vals[:, pl.ds(pl.multiple_of(n * CHUNK, CHUNK), CHUNK)]
        at_row = number == v[3:4]
        at_lane = jnp.where(number == v[7:8], 1.0, 0.0).astype(BF16)
        picked = jnp.dot(
            tabs[...], jnp.concatenate([at_lane, at_lane], axis=0), preferred_element_type=F32
        )

        def value(m):
            return jnp.sum(
                jnp.where(at_row, picked[128 * m : 128 * m + 128], 0.0), axis=0, keepdims=True
            )

        slip = (value(2) - v[4:5]) ** 2 + (value(3) - v[5:6]) ** 2 + (value(4) - v[6:7]) ** 2
        coef = v[0:1] * jnp.sqrt(1.0 + slip)
        rate = coef * (v[1:2] - value(0))
        heat = coef * (v[2:3] - value(1)) - LATENT * rate
        rows = []
        for x in (rate, heat):
            first = x.astype(BF16).astype(F32)
            rows.append(jnp.where(at_row, first, 0.0).astype(BF16))
            rows.append(jnp.where(at_row, x - first, 0.0).astype(BF16))
        return acc + lax.dot_general(
            jnp.concatenate(rows, axis=0),
            at_lane,
            (((1,), (1,)), ((), ())),
            preferred_element_type=F32,
        )

    return lax.fori_loop(low, high, add_chunk, acc)


def deposit_end(acc, new_ref):
    fuel = (acc[0:128] + acc[128:256]).reshape(BE, 8, 128)
    heat = (acc[256:384] + acc[384:512]).reshape(BE, 8, 128)
    new_ref[0] = new_ref[0] + DEPOSIT * fuel
    new_ref[FIELDS - 1] = new_ref[FIELDS - 1] + DEPOSIT * heat


def to_tiles(array):
    fields = array.shape[0]
    return (
        array.reshape(fields, 4, 32, 128).transpose(0, 2, 1, 3).reshape(fields, BE, 8, 128)
    )


def from_tiles(array):
    fields = array.shape[0]
    return array.reshape(fields, 32, 4, 128).transpose(0, 2, 1, 3).reshape(fields, 4, 4096)


def per_device(
    state,
    velocity,
    history,
    diffusion,
    box_target,
    parcel_mass,
    parcel_state,
    parcel_box,
    parcel_cell,
    parcel_count,
):
    new_state, tendency = step(
        to_tiles(state),
        to_tiles(velocity),
        to_tiles(history),
        diffusion,
        box_target,
        parcel_mass[None],
        parcel_state,
        parcel_box[None],
        parcel_cell[None],
        parcel_count,
    )
    new_state, tendency = hand_over(new_state, tendency)
    return from_tiles(new_state), from_tiles(tendency)


def solution(mesh):
    return jax.shard_map(
        per_device,
        mesh=mesh,
        in_specs=(
            P(None, ("slab", "cross"), None),
            P(None, ("slab", "cross"), None),
            P(None, ("slab", "cross"), None),
            P(),
            P("slab", "cross"),
            P(("slab", "cross")),
            P(None, ("slab", "cross")),
            P(("slab", "cross")),
            P(("slab", "cross")),
            P(("slab", "cross")),
        ),
        out_specs=(P(None, ("slab", "cross"), None), P(None, ("slab", "cross"), None)),
        check_vma=False,
    )
```

```python
import jax
import jax.numpy as jnp
from jax import lax
from jax.experimental import pallas as pl
from jax.experimental.pallas import tpu as pltpu
from jax.sharding import PartitionSpec as P

MESH = pl.DeviceIdType.MESH
F32 = jnp.float32
BF16 = jnp.bfloat16

BE = 16
PAR_DEV = 4096
CAP = 64
FIELDS = 22
N_SLAB = 8
N_CROSS = 16
CHUNK = 512
VMEM_LIMIT = 54 * 2**20

TIME_STEP = 0.2
LATENT = 0.5
DEPOSIT = 0.25

GROUPS = (
    ((1, 0, 3), (0, 0, 4)),
    ((0, 4, 6),),
    ((0, 10, 6),),
    ((0, 16, 6), (2, 0, 1), (2, 21, 1)),
    ((2, 1, 5),),
    ((2, 6, 5),),
    ((2, 11, 5),),
    ((2, 16, 5),),
)
WIDTHS = tuple(sum(part[2] for part in group) for group in GROUPS)
N_GAS = 4
GAS = tuple(sum(part[2] for part in group if part[0] < 2) for group in GROUPS[:N_GAS])

SCHEDULE = (
    ("1", 0), ("1", 1), ("1", 2), ("1", 3),
    ("pack", 0), ("invert", 0),
    ("2", 0), ("2", 1), ("2", 2), ("2", 3), ("pass", 0),
    ("landed", 0), ("landed", 1), ("1", 4), ("landed", 2), ("landed", 3),
    ("halo", 0), ("1", 5), ("1", 6), ("1", 7), ("faces", 0), ("sweep", 0), ("sweep", 1), ("sweep", 2), ("sweep", 3), ("2", 4), ("2", 5), ("2", 6), ("2", 7),
    ("advance", 3), ("parcels", 0), ("chunks", 0), ("chunks", 1), ("chunks", 2), ("chunks", 3), ("deposit", 0),
    ("landed", 4), ("advance", 4), ("landed", 5), ("advance", 5), ("landed", 6), ("advance", 6), ("landed", 7), ("advance", 7),
)


def runs(which):
    found = []
    for g, group in enumerate(GROUPS):
        row = 0
        for source, first, count in group:
            if source == which:
                found.append((first, count, g, row))
            row += count
    return sorted(found)


def place_of(which, field):
    for first, count, g, row in runs(which):
        if first <= field < first + count:
            return g, row + field - first, first + count - field


def iota(dim, shape=(8, 128)):
    return lax.broadcasted_iota(jnp.int32, shape, dim)


def lane_roll(x, shift):
    shift = shift % 128
    return x if shift == 0 else pltpu.roll(x, shift, x.ndim - 1)


def sub_roll(x, shift):
    shift = shift % 8
    return x if shift == 0 else pltpu.roll(x, shift, x.ndim - 2)


def pack(mass, parcels, box, cell, count, w, spans_v, spans_s, sem, out):
    def columns(n, carry):
        at = pl.ds(pl.multiple_of(n * 128, 128), 128)
        w[n, 0:1] = mass[:, at]
        w[n, 1:3] = parcels[0:2, at]
        w[n, 3:4] = ((cell[:, at] // 128) * 4 + box[:, at] % 4).astype(F32)
        w[n, 4:7] = parcels[2:5, at]
        w[n, 7:8] = (cell[:, at] % 128).astype(F32)
        return carry

    lax.fori_loop(0, PAR_DEV // 128, columns, 0, unroll=2)
    w[PAR_DEV // 128] = jnp.zeros((8, 128), F32)

    shape = (N_SLAB * N_CROSS, 128)
    number = iota(0, shape)
    lane = iota(1, shape)
    live = count[0]

    def scan(n, carry):
        first, length = carry
        owner = box[:, pl.ds(pl.multiple_of(n * 128, 128), 128)] // 4
        here = owner == number
        position = lane + n * 128
        first = jnp.where(here, jnp.minimum(first, position), first)
        length = length + jnp.where(here & (position < live), 1, 0)
        return first, length

    first, length = lax.fori_loop(
        0,
        PAR_DEV // 128,
        scan,
        (jnp.full(shape, PAR_DEV - 1, jnp.int32), jnp.zeros(shape, jnp.int32)),
    )
    first = jnp.min(first, axis=1, keepdims=True)
    length = jnp.sum(length, axis=1, keepdims=True)
    spans_v[...] = jnp.where(lane == 0, first, length)
    copy = pltpu.make_async_copy(spans_v, spans_s, sem)
    copy.start()
    copy.wait()

    lane = iota(1)
    row = iota(0)

    def body(o, carry):
        start = spans_s[o, 0] & (PAR_DEV - 1)
        tile = lax.div(start, 128)
        first, second = w[tile], w[tile + 1]
        offset = jnp.full((8, 128), start, jnp.int32)
        ahead = pltpu.roll(jnp.where(lane < 64, second, first), 64, 1)
        window = jnp.where((offset & 64) != 0, ahead, first)
        for bit in (32, 16, 8, 4, 2, 1):
            window = jnp.where((offset & bit) != 0, pltpu.roll(window, 128 - bit, 1), window)
        window = jnp.where((row == 0) & (lane >= spans_s[o, 1]), 0.0, window)
        low = window[0:4]
        high = pltpu.roll(window, 64, 1)[4:8]
        out[o % N_CROSS, o // N_CROSS] = jnp.where(lane[0:4] < 64, low, high)
        return carry

    lax.fori_loop(0, N_SLAB * N_CROSS, body, 0, unroll=8)


def step_kernel(
    s_ref, v_ref, h_ref, d_ref, tg_ref, mass_hbm, ps_hbm, box_hbm, cell_hbm, count_ref,
    new_ref, tend_ref,
    *scratch,
):
    arrays = (s_ref, v_ref, h_ref)
    n = len(GROUPS)
    bufs, outs, placed = scratch[0:n], scratch[n : 2 * n], scratch[2 * n : 3 * n]
    scratch = scratch[3 * n :]
    (xl, xh, zl, zh, z0, z15) = scratch[0:6]
    (sb, r1, r2) = scratch[6:9]
    (tgv, tgb, inv_v, inv_s, w, spans_v, spans_s) = scratch[9:16]
    (gx, hx, gy, hy, gz, hz, gzp, hzp, vals, tabs) = scratch[16:26]
    (tsem, p1, p2, hsem, psem, lsem) = scratch[26:32]
    (mass_ref, ps_ref, box_ref, cell_ref, isem) = scratch[32:37]

    fetches = [
        pltpu.make_async_copy(src, dst, isem.at[k])
        for k, (src, dst) in enumerate(
            (
                (mass_hbm, mass_ref),
                (ps_hbm, ps_ref),
                (box_hbm, box_ref),
                (cell_hbm, cell_ref),
            )
        )
    ]
    for fetch in fetches:
        fetch.start()

    me_s = lax.axis_index("slab")
    me_c = lax.axis_index("cross")

    me_x, me_z = lax.div(me_c, 4), lax.rem(me_c, 4)

    def cross(d):
        return lax.rem(me_x + lax.div(d, 4), 4) * 4 + lax.rem(me_z + lax.rem(d, 4), 4)

    def slab(d):
        return lax.rem(me_s + d, N_SLAB)

    barrier = pltpu.get_barrier_semaphore()

    def greet_c(d, carry):
        pl.semaphore_signal(barrier, inc=1, device_id=(me_s, cross(d)), device_id_type=MESH)
        return carry

    def greet_s(d, carry):
        pl.semaphore_signal(barrier, inc=1, device_id=(slab(d), me_c), device_id_type=MESH)
        return carry

    lax.fori_loop(1, N_CROSS, greet_c, 0)
    lax.fori_loop(1, N_SLAB, greet_s, 0)
    pl.semaphore_wait(barrier, N_CROSS - 1 + N_SLAB - 1)

    def remote(src, dst, sems, peer):
        return pltpu.make_async_remote_copy(
            src_ref=src,
            dst_ref=dst,
            send_sem=sems.at[0],
            recv_sem=sems.at[1],
            device_id=peer,
            device_id_type=MESH,
        )

    def drain(ref, sem):
        pltpu.make_async_copy(ref, ref, sem).wait()

    mine = jnp.zeros((8, 128), jnp.int32)
    for k in range(4):
        mine = mine + jnp.where(iota(1) == 4 * me_c + k, tg_ref[0, k], 0)
    tgv[...] = mine
    tgb[me_c] = mine

    def send_targets(d, carry):
        remote(tgv, tgb.at[me_c], tsem, (me_s, cross(d))).start()
        return carry

    lax.fori_loop(1, N_CROSS, send_targets, 0)

    def parts(g):
        at = 0
        for which, first, count in GROUPS[g]:
            yield arrays[which], first, count, at
            at += count

    def phase1(g):
        sems = p1.at[g]

        def body(d, carry):
            m = cross(d)
            for src, first, count, at in parts(g):
                remote(
                    src.at[pl.ds(first, count), m],
                    bufs[g].at[me_c, pl.ds(at, count)],
                    sems,
                    (me_s, m),
                ).start()
            return carry

        lax.fori_loop(1, N_CROSS, body, 0)
        for src, first, count, at in parts(g):
            pltpu.make_async_copy(
                src.at[pl.ds(first, count), me_c], bufs[g].at[me_c, pl.ds(at, count)], lsem.at[g]
            ).start()

    def phase2(g):
        width = WIDTHS[g]
        sems = p1.at[g]
        drain(bufs[g].at[pl.ds(0, N_CROSS - 1)], sems.at[1])
        drain(bufs[g].at[0], lsem.at[g])

        def fill(t):
            for q in range(4):
                code = inv_s[t * 4 + q, 0] & 63
                outs[g][t, :, q : q + 5 : 4, :] = bufs[g][
                    lax.div(code, 4), :, pl.ds(lax.rem(code, 4), 2, stride=4), :
                ]

        def body(d, carry):
            t = cross(d)
            fill(t)
            remote(outs[g].at[t], placed[g].at[me_c], p2.at[g], (me_s, t)).start()
            return carry

        lax.fori_loop(1, N_CROSS, body, 0)
        fill(me_c)
        pltpu.make_async_copy(outs[g].at[me_c], placed[g].at[me_c], lsem.at[g]).start()

    def landed(g):
        drain(placed[g].at[pl.ds(0, N_CROSS - 1)], p2.at[g, 1])
        drain(placed[g].at[0], lsem.at[g])

    def sent(g):
        drain(bufs[g].at[pl.ds(0, N_CROSS - 1)], p1.at[g, 0])
        drain(outs[g].at[pl.ds(0, N_CROSS - 1)], p2.at[g, 0])

    def invert():
        drain(tgb.at[pl.ds(0, N_CROSS - 1)], tsem.at[1])
        flat = tgb[0]
        for s in range(1, N_CROSS):
            flat = flat + tgb[s]
        for tile in range(8):
            hit = flat == iota(0) + 8 * tile
            code = jnp.sum(jnp.where(hit & (iota(1) < 64), iota(1), 0), axis=1, keepdims=True)
            inv_v[8 * tile : 8 * tile + 8, :] = jnp.broadcast_to(code, (8, 128))
        to_scalar = pltpu.make_async_copy(inv_v, inv_s, lsem.at[n])
        to_scalar.start()
        to_scalar.wait()

    halo = []

    def send_halos():
        x_lo = (me_s, lax.rem(me_c + N_CROSS - 1, N_CROSS))
        x_hi = (me_s, lax.rem(me_c + 1, N_CROSS))
        for g in range(N_GAS):
            at = pl.ds(sum(GAS[:g]), GAS[g])
            rows = pl.ds(0, GAS[g])
            halo.append(remote(placed[g].at[0, rows], xh.at[at], hsem.at[2 * g], x_lo))
            halo.append(remote(placed[g].at[BE - 1, rows], xl.at[at], hsem.at[2 * g + 1], x_hi))
        for copy in halo:
            copy.start()
        pack_z(placed, z0, z15)
        z_lo = (slab(N_SLAB - 1), me_c)
        z_hi = (slab(1), me_c)
        for copy in (
            remote(z0, zh, hsem.at[2 * N_GAS], z_lo),
            remote(z15, zl, hsem.at[2 * N_GAS + 1], z_hi),
        ):
            copy.start()
            halo.append(copy)

    def parcels1(d, carry):
        c = cross(d)
        remote(sb.at[c], r1.at[me_c], psem.at[0], (me_s, c)).start()
        return carry

    def parcels2(d, carry):
        a = slab(d)
        remote(r1.at[:, a], r2.at[me_s], psem.at[1], (a, me_c)).start()
        return carry

    kept = {}
    chunks = N_SLAB * N_CROSS * CAP // CHUNK
    for name, g in SCHEDULE:
        if name == "1":
            phase1(g)
        elif name == "2":
            phase2(g)
        elif name == "landed":
            landed(g)
        elif name == "pack":
            for fetch in fetches:
                fetch.wait()
            pack(mass_ref, ps_ref, box_ref, cell_ref, count_ref, w, spans_v, spans_s, lsem.at[n], sb)
            lax.fori_loop(1, N_CROSS, parcels1, 0)
            own = pltpu.make_async_copy(sb.at[me_c], r1.at[me_c], lsem.at[n])
            own.start()
            own.wait()
        elif name == "invert":
            invert()
        elif name == "pass":
            drain(r1.at[pl.ds(0, N_CROSS - 1)], psem.at[0, 1])
            lax.fori_loop(1, N_SLAB, parcels2, 0)
            own = pltpu.make_async_copy(r1.at[:, me_s], r2.at[me_s], lsem.at[n])
            own.start()
            own.wait()
        elif name == "halo":
            send_halos()
        elif name == "faces":
            for copy in halo:
                copy.wait()
            kept["sweep"] = faces(
                d_ref, placed, xl, xh, zl, zh, z0, z15, tend_ref,
                gx, hx, gy, hy, gz, hz, gzp, hzp,
            )
        elif name == "sweep":
            kept["sweep"](g)
        elif name == "advance":
            advance(placed, g, tend_ref, new_ref)
        elif name == "parcels":
            drain(r2.at[pl.ds(0, N_SLAB - 1)], psem.at[1, 1])
            deposit_start(placed[0], r2, new_ref, vals, tabs)
            kept["acc"] = jnp.zeros((512, 128), F32)
        elif name == "chunks":
            low, high = chunks * g // 4, chunks * (g + 1) // 4
            kept["acc"] = deposit_chunks(low, high, kept["acc"], vals, tabs)
        elif name == "deposit":
            deposit_end(kept["acc"], new_ref)

    drain(tgb.at[pl.ds(0, N_CROSS - 1)], tsem.at[0])
    drain(r1.at[pl.ds(0, N_CROSS - 1)], psem.at[0, 0])
    drain(r2.at[pl.ds(0, N_SLAB - 1)], psem.at[1, 0])
    for g in range(n):
        sent(g)


def pack_z(placed, z0, z15):
    lane16 = iota(1) // 16
    upper = iota(0) >= 4

    for g in range(N_GAS):
        first = sum(GAS[:g])

        def body(f, carry):
            low = [None, None]
            high = [None, None]
            for ih in range(2):
                for il in range(8):
                    x = placed[g][ih * 8 + il, f]
                    a = lane_roll(x, 16 * il)
                    b = lane_roll(x, 16 * il + 16)
                    if il == 0:
                        low[ih], high[ih] = a, b
                    else:
                        low[ih] = jnp.where(lane16 == il, a, low[ih])
                        high[ih] = jnp.where(lane16 == il, b, high[ih])
            z0[first + f] = jnp.where(upper, sub_roll(low[1], 4), low[0])
            z15[first + f] = jnp.where(upper, high[1], sub_roll(high[0], 4))
            return carry

        lax.fori_loop(0, GAS[g], body, 0)


def step(state, velocity, history, diffusion, targets, mass, parcels, box, cell, count):
    vm = pl.BlockSpec(memory_space=pltpu.VMEM)
    sm = pl.BlockSpec(memory_space=pltpu.SMEM)
    hbm = pl.BlockSpec(memory_space=pl.ANY)
    group = [(N_CROSS, w, 8, 128) for w in WIDTHS]
    devices = N_SLAB * N_CROSS
    out = jax.ShapeDtypeStruct((FIELDS, BE, 8, 128), F32)
    return pl.pallas_call(
        step_kernel,
        out_shape=[pltpu.VMEM((FIELDS, BE, 8, 128), F32)] * 2,
        in_specs=[hbm, hbm, hbm, sm, sm, hbm, hbm, hbm, hbm, sm],
        out_specs=[vm, vm],
        scratch_shapes=[pltpu.VMEM(s, F32) for s in group * 3]
        + [pltpu.VMEM((sum(GAS), 8, 128), F32)] * 6
        + [pltpu.VMEM((N_CROSS, N_SLAB, 4, 128), F32)] * 2
        + [pltpu.VMEM((N_SLAB, N_CROSS, 4, 128), F32)]
        + [
            pltpu.VMEM((8, 128), jnp.int32),
            pltpu.VMEM((N_CROSS, 8, 128), jnp.int32),
            pltpu.VMEM((64, 128), jnp.int32),
            pltpu.SMEM((64, 128), jnp.int32),
            pltpu.VMEM((PAR_DEV // 128 + 1, 8, 128), F32),
            pltpu.VMEM((devices, 128), jnp.int32),
            pltpu.SMEM((devices, 128), jnp.int32),
        ]
        + [pltpu.VMEM((BE + 1, 8, 128), F32)] * 2
        + [pltpu.VMEM((BE, 8, 128), F32)] * 4
        + [pltpu.VMEM((2, 8, 128), F32)] * 2
        + [pltpu.VMEM((8, devices * CAP), F32), pltpu.VMEM((640, 256), BF16)]
        + [
            pltpu.SemaphoreType.DMA((2,)),
            pltpu.SemaphoreType.DMA((len(GROUPS), 2)),
            pltpu.SemaphoreType.DMA((len(GROUPS), 2)),
            pltpu.SemaphoreType.DMA((2 * N_GAS + 2, 2)),
            pltpu.SemaphoreType.DMA((2, 2)),
            pltpu.SemaphoreType.DMA((len(GROUPS) + 1,)),
            pltpu.VMEM((1, PAR_DEV), F32),
            pltpu.VMEM((5, PAR_DEV), F32),
            pltpu.VMEM((1, PAR_DEV), jnp.int32),
            pltpu.VMEM((1, PAR_DEV), jnp.int32),
            pltpu.SemaphoreType.DMA((4,)),
        ],
        compiler_params=pltpu.CompilerParams(
            collective_id=0, has_side_effects=True, vmem_limit_bytes=VMEM_LIMIT
        ),
    )(state, velocity, history, diffusion, targets, mass, parcels, box, cell, count)


def hand_over_kernel(a_ref, b_ref, a_out, b_out, sems):
    copies = []
    for k, (src, dst) in enumerate(((a_ref, a_out), (b_ref, b_out))):
        for part in range(2):
            at = pl.ds(part * (FIELDS // 2), FIELDS // 2)
            copies.append(pltpu.make_async_copy(src.at[at], dst.at[at], sems.at[2 * k + part]))
    for copy in copies:
        copy.start()
    for copy in copies:
        copy.wait()


def hand_over(a, b):
    out = jax.ShapeDtypeStruct((FIELDS, BE, 8, 128), F32)
    return pl.pallas_call(
        hand_over_kernel,
        out_shape=[out, out],
        in_specs=[pl.BlockSpec(memory_space=pl.ANY)] * 2,
        out_specs=[pl.BlockSpec(memory_space=pl.ANY)] * 2,
        scratch_shapes=[pltpu.SemaphoreType.DMA((4,))],
        compiler_params=pltpu.CompilerParams(vmem_limit_bytes=8 * 2**20),
    )(a, b)


def spread_of(e):
    return 1.0 + 0.5 * jnp.tanh(e)


def faces(
    d_ref, placed, xl, xh, zl, zh, z0, z15, tend_ref, gx, hx, gy, hy, gz, hz, gzp, hzp
):
    me_c = lax.axis_index("cross")
    lane = iota(1)
    row = iota(0)
    kl7 = lane >= 112
    kl0 = lane < 16
    top = kl7 & (row >= 4)
    bottom = kl0 & (row < 4)
    j15 = lane % 16 == 15
    j0 = lane % 16 == 0
    wall_y = j15 & (row % 4 == 3)

    def up_z(q):
        return lane_roll(jnp.where(kl0, sub_roll(q, 4), q), -16)

    def down_z(q):
        return lane_roll(jnp.where(kl7, sub_roll(q, 4), q), 16)

    def up_y(q):
        return jnp.where(j15, sub_roll(lane_roll(q, 15), -1), lane_roll(q, -1))

    def down_y(q):
        return jnp.where(j0, sub_roll(lane_roll(q, -15), 1), lane_roll(q, 1))

    def put_top(packed, i):
        ih, il = divmod(i, 8)
        return lane_roll(packed[1 - ih], 112 - 16 * il)

    def put_bottom(packed, i):
        ih, il = divmod(i, 8)
        return lane_roll(packed[ih], -16 * il)

    p0 = placed[0]
    pe, E, _ = place_of(0, FIELDS - 1)
    EH = sum(GAS[:pe]) + E
    pe = placed[pe]
    first_wall = jnp.where(me_c == 0, 0.0, 1.0)
    last_wall = jnp.where(me_c == N_CROSS - 1, 0.0, 1.0)
    before_g = spread_of(xl[EH])
    before_u = xl[0]
    for i in range(BE + 1):
        if i < BE:
            now_g, now_u = spread_of(pe[i, E]), p0[i, 0]
        else:
            now_g, now_u = spread_of(xh[EH]), xh[0]
        g, h = 0.5 * (before_g + now_g), 0.25 * (before_u + now_u)
        if i == 0:
            g, h = g * first_wall, h * first_wall
        if i == BE:
            g, h = g * last_wall, h * last_wall
        gx[i], hx[i] = g, h
        before_g, before_u = now_g, now_u
        if i < BE:
            uy, uz = p0[i, 1], p0[i, 2]
            gy[i] = jnp.where(wall_y, 0.0, 0.5 * (now_g + up_y(now_g)))
            hy[i] = jnp.where(wall_y, 0.0, 0.25 * (uy + up_y(uy)))
            gz[i] = 0.5 * (now_g + up_z(now_g))
            hz[i] = 0.25 * (uz + up_z(uz))
    gzp[0] = 0.5 * (spread_of(zl[EH]) + spread_of(z0[EH]))
    gzp[1] = 0.5 * (spread_of(z15[EH]) + spread_of(zh[EH]))
    hzp[0] = 0.25 * (zl[2] + z0[2])
    hzp[1] = 0.25 * (z15[2] + zh[2])

    def flux(d, g, h, low, high):
        return (d * g) * (high - low) - h * (high + low)

    def sweep(q_ref, q_at, x_at, out_at, count):
        def body(n, carry):
            f = out_at + n
            d = d_ref[f]
            xf = x_at + n
            qf = q_at + n
            edge0 = flux(d, gzp[0], hzp[0], zl[xf], z0[xf])
            edge15 = flux(d, gzp[1], hzp[1], z15[xf], zh[xf])
            edge0 = (edge0, sub_roll(edge0, 4))
            edge15 = (edge15, sub_roll(edge15, 4))
            q = q_ref[0, qf]
            fx = flux(d, gx[0], hx[0], xl[xf], q)
            for i in range(BE):
                ahead = q_ref[i + 1, qf] if i < BE - 1 else xh[xf]
                fx_up = flux(d, gx[i + 1], hx[i + 1], q, ahead)
                total = fx_up - fx
                fz = flux(d, gz[i], hz[i], q, up_z(q))
                fz = jnp.where(top, put_top(edge15, i), fz)
                fz_low = jnp.where(bottom, put_bottom(edge0, i), down_z(fz))
                total = total + fz - fz_low
                fy = flux(d, gy[i], hy[i], q, up_y(q))
                total = total + fy - down_y(fy)
                tend_ref[f, i] = total
                fx = fx_up
                q = ahead
            return carry

        lax.fori_loop(0, count, body, 0)

    def sweep_group(g):
        for first, count, group, row in runs(0):
            if group == g:
                sweep(placed[g], row, sum(GAS[:g]) + row, first, count)

    return sweep_group


def advance(placed, g, tend_ref, new_ref):
    for first, count, group, h_row in runs(2):
        if group != g:
            continue
        f = first
        while f < first + count:
            q_group, q_row, left = place_of(0, f)
            many = min(left, first + count - f)
            advance_run(placed[q_group], q_row, placed[g], h_row + f - first, tend_ref, new_ref, f, many)
            f += many


def advance_run(q_ref, q_at, h_ref, h_at, tend_ref, new_ref, f_at, count):
    def body(m, carry):
        new_ref[f_at + m] = q_ref[:, q_at + m] + TIME_STEP * (
            1.5 * tend_ref[f_at + m] - 0.5 * h_ref[:, h_at + m]
        )
        return carry

    lax.fori_loop(0, count, body, 0)


def deposit_start(p0, r2, new_ref, vals, tabs):
    tables = [new_ref[0], new_ref[FIELDS - 1]] + [p0[:, d] for d in range(3)]
    for n, table in enumerate(tables):
        table = table.reshape(128, 128)
        first = table.astype(BF16)
        tabs[128 * n : 128 * n + 128, 0:128] = first
        tabs[128 * n : 128 * n + 128, 128:256] = (table - first.astype(F32)).astype(BF16)

    half = iota(1, (4, 128)) < 64

    def unpack(n, carry):
        a, b = r2[n // 8, 2 * (n % 8)], r2[n // 8, 2 * (n % 8) + 1]
        at = pl.ds(pl.multiple_of(n * 128, 128), 128)
        vals[0:4, at] = jnp.where(half, a, pltpu.roll(b, 64, 1))
        vals[4:8, at] = jnp.where(half, pltpu.roll(a, 64, 1), b)
        return carry

    lax.fori_loop(0, 64, unpack, 0, unroll=4)


def deposit_chunks(low, high, acc, vals, tabs):
    number = lax.broadcasted_iota(jnp.int32, (128, CHUNK), 0).astype(F32)

    def add_chunk(n, acc):
        v = vals[:, pl.ds(pl.multiple_of(n * CHUNK, CHUNK), CHUNK)]
        at_row = number == v[3:4]
        at_lane = jnp.where(number == v[7:8], 1.0, 0.0).astype(BF16)
        picked = jnp.dot(
            tabs[...], jnp.concatenate([at_lane, at_lane], axis=0), preferred_element_type=F32
        )

        def value(m):
            return jnp.sum(
                jnp.where(at_row, picked[128 * m : 128 * m + 128], 0.0), axis=0, keepdims=True
            )

        slip = (value(2) - v[4:5]) ** 2 + (value(3) - v[5:6]) ** 2 + (value(4) - v[6:7]) ** 2
        coef = v[0:1] * jnp.sqrt(1.0 + slip)
        rate = coef * (v[1:2] - value(0))
        heat = coef * (v[2:3] - value(1)) - LATENT * rate
        rows = []
        for x in (rate, heat):
            first = x.astype(BF16).astype(F32)
            rows.append(jnp.where(at_row, first, 0.0).astype(BF16))
            rows.append(jnp.where(at_row, x - first, 0.0).astype(BF16))
        return acc + lax.dot_general(
            jnp.concatenate(rows, axis=0),
            at_lane,
            (((1,), (1,)), ((), ())),
            preferred_element_type=F32,
        )

    return lax.fori_loop(low, high, add_chunk, acc)


def deposit_end(acc, new_ref):
    fuel = (acc[0:128] + acc[128:256]).reshape(BE, 8, 128)
    heat = (acc[256:384] + acc[384:512]).reshape(BE, 8, 128)
    new_ref[0] = new_ref[0] + DEPOSIT * fuel
    new_ref[FIELDS - 1] = new_ref[FIELDS - 1] + DEPOSIT * heat


def to_tiles(array):
    fields = array.shape[0]
    return (
        array.reshape(fields, 4, 32, 128).transpose(0, 2, 1, 3).reshape(fields, BE, 8, 128)
    )


def from_tiles(array):
    fields = array.shape[0]
    return array.reshape(fields, 32, 4, 128).transpose(0, 2, 1, 3).reshape(fields, 4, 4096)


def per_device(
    state,
    velocity,
    history,
    diffusion,
    box_target,
    parcel_mass,
    parcel_state,
    parcel_box,
    parcel_cell,
    parcel_count,
):
    new_state, tendency = step(
        to_tiles(state),
        to_tiles(velocity),
        to_tiles(history),
        diffusion,
        box_target,
        parcel_mass[None],
        parcel_state,
        parcel_box[None],
        parcel_cell[None],
        parcel_count,
    )
    new_state, tendency = hand_over(new_state, tendency)
    return from_tiles(new_state), from_tiles(tendency)


def solution(mesh):
    return jax.shard_map(
        per_device,
        mesh=mesh,
        in_specs=(
            P(None, ("slab", "cross"), None),
            P(None, ("slab", "cross"), None),
            P(None, ("slab", "cross"), None),
            P(),
            P("slab", "cross"),
            P(("slab", "cross")),
            P(None, ("slab", "cross")),
            P(("slab", "cross")),
            P(("slab", "cross")),
            P(("slab", "cross")),
        ),
        out_specs=(P(None, ("slab", "cross"), None), P(None, ("slab", "cross"), None)),
        check_vma=False,
    )
```

```python
import jax
import jax.numpy as jnp
from jax import lax
from jax.experimental import pallas as pl
from jax.experimental.pallas import tpu as pltpu
from jax.sharding import PartitionSpec as P

MESH = pl.DeviceIdType.MESH
F32 = jnp.float32
BF16 = jnp.bfloat16

BE = 16
PAR_DEV = 4096
CAP = 64
FIELDS = 22
N_SLAB = 8
N_CROSS = 16
CHUNK = 512
VMEM_LIMIT = 54 * 2**20

TIME_STEP = 0.2
LATENT = 0.5
DEPOSIT = 0.25

GROUPS = (
    ((1, 0, 3), (0, 0, 4)),
    ((0, 4, 6),),
    ((0, 10, 6),),
    ((0, 16, 6), (2, 0, 1), (2, 21, 1)),
    ((2, 1, 5),),
    ((2, 6, 5),),
    ((2, 11, 5),),
    ((2, 16, 5),),
)
WIDTHS = tuple(sum(part[2] for part in group) for group in GROUPS)
N_GAS = 4
GAS = tuple(sum(part[2] for part in group if part[0] < 2) for group in GROUPS[:N_GAS])

SCHEDULE = (
    ("1", 0), ("1", 1), ("1", 2), ("1", 3),
    ("pack", 0), ("invert", 0),
    ("2", 0), ("2", 1), ("2", 2), ("2", 3), ("pass", 0),
    ("landed", 0), ("landed", 1), ("1", 4), ("landed", 2), ("landed", 3),
    ("halo", 0), ("1", 5), ("1", 6), ("1", 7), ("faces", 0), ("sweep", 0), ("sweep", 1), ("sweep", 2), ("sweep", 3), ("2", 4), ("2", 5), ("2", 6), ("2", 7),
    ("advance", 3), ("parcels", 0), ("chunks", 0), ("chunks", 1), ("chunks", 2), ("chunks", 3), ("deposit", 0),
    ("landed", 4), ("advance", 4), ("landed", 5), ("advance", 5), ("landed", 6), ("advance", 6), ("landed", 7), ("advance", 7),
)


def runs(which):
    found = []
    for g, group in enumerate(GROUPS):
        row = 0
        for source, first, count in group:
            if source == which:
                found.append((first, count, g, row))
            row += count
    return sorted(found)


def place_of(which, field):
    for first, count, g, row in runs(which):
        if first <= field < first + count:
            return g, row + field - first, first + count - field


def iota(dim, shape=(8, 128)):
    return lax.broadcasted_iota(jnp.int32, shape, dim)


def lane_roll(x, shift):
    shift = shift % 128
    return x if shift == 0 else pltpu.roll(x, shift, x.ndim - 1)


def sub_roll(x, shift):
    shift = shift % 8
    return x if shift == 0 else pltpu.roll(x, shift, x.ndim - 2)


def pack(mass, parcels, box, cell, count, w, spans_v, spans_s, sem, out):
    def columns(n, carry):
        at = pl.ds(pl.multiple_of(n * 128, 128), 128)
        w[n, 0:1] = mass[:, at]
        w[n, 1:3] = parcels[0:2, at]
        w[n, 3:4] = ((cell[:, at] // 128) * 4 + box[:, at] % 4).astype(F32)
        w[n, 4:7] = parcels[2:5, at]
        w[n, 7:8] = (cell[:, at] % 128).astype(F32)
        return carry

    lax.fori_loop(0, PAR_DEV // 128, columns, 0, unroll=2)
    w[PAR_DEV // 128] = jnp.zeros((8, 128), F32)

    shape = (N_SLAB * N_CROSS, 128)
    number = iota(0, shape)
    lane = iota(1, shape)
    live = count[0]

    def scan(n, carry):
        first, length = carry
        owner = box[:, pl.ds(pl.multiple_of(n * 128, 128), 128)] // 4
        here = owner == number
        position = lane + n * 128
        first = jnp.where(here, jnp.minimum(first, position), first)
        length = length + jnp.where(here & (position < live), 1, 0)
        return first, length

    first, length = lax.fori_loop(
        0,
        PAR_DEV // 128,
        scan,
        (jnp.full(shape, PAR_DEV - 1, jnp.int32), jnp.zeros(shape, jnp.int32)),
    )
    first = jnp.min(first, axis=1, keepdims=True)
    length = jnp.sum(length, axis=1, keepdims=True)
    spans_v[...] = jnp.where(lane == 0, first, length)
    copy = pltpu.make_async_copy(spans_v, spans_s, sem)
    copy.start()
    copy.wait()

    lane = iota(1)
    row = iota(0)

    def body(o, carry):
        start = spans_s[o, 0] & (PAR_DEV - 1)
        tile = lax.div(start, 128)
        first, second = w[tile], w[tile + 1]
        offset = jnp.full((8, 128), start, jnp.int32)
        ahead = pltpu.roll(jnp.where(lane < 64, second, first), 64, 1)
        window = jnp.where((offset & 64) != 0, ahead, first)
        for bit in (32, 16, 8, 4, 2, 1):
            window = jnp.where((offset & bit) != 0, pltpu.roll(window, 128 - bit, 1), window)
        window = jnp.where((row == 0) & (lane >= spans_s[o, 1]), 0.0, window)
        low = window[0:4]
        high = pltpu.roll(window, 64, 1)[4:8]
        out[o % N_CROSS, o // N_CROSS] = jnp.where(lane[0:4] < 64, low, high)
        return carry

    lax.fori_loop(0, N_SLAB * N_CROSS, body, 0, unroll=8)


def step_kernel(
    s_ref, v_ref, h_ref, d_ref, tg_ref, mass_hbm, ps_hbm, box_hbm, cell_hbm, count_ref,
    new_ref, tend_ref,
    *scratch,
):
    arrays = (s_ref, v_ref, h_ref)
    n = len(GROUPS)
    bufs, outs, placed = scratch[0:n], scratch[n : 2 * n], scratch[2 * n : 3 * n]
    scratch = scratch[3 * n :]
    (xl, xh, zl, zh, z0, z15) = scratch[0:6]
    (sb, r1, r2) = scratch[6:9]
    (tgv, tgb, inv_v, inv_s, w, spans_v, spans_s) = scratch[9:16]
    (gx, hx, gy, hy, gz, hz, gzp, hzp, vals, tabs) = scratch[16:26]
    (tsem, p1, p2, hsem, psem, lsem) = scratch[26:32]
    (mass_ref, ps_ref, box_ref, cell_ref, isem) = scratch[32:37]

    fetches = [
        pltpu.make_async_copy(src, dst, isem.at[k])
        for k, (src, dst) in enumerate(
            (
                (mass_hbm, mass_ref),
                (ps_hbm, ps_ref),
                (box_hbm, box_ref),
                (cell_hbm, cell_ref),
            )
        )
    ]
    for fetch in fetches:
        fetch.start()

    me_s = lax.axis_index("slab")
    me_c = lax.axis_index("cross")

    me_x, me_z = lax.div(me_c, 4), lax.rem(me_c, 4)

    def cross(d):
        return lax.rem(me_x + lax.div(d, 4), 4) * 4 + lax.rem(me_z + lax.rem(d, 4), 4)

    def slab(d):
        return lax.rem(me_s + d, N_SLAB)

    barrier = pltpu.get_barrier_semaphore()

    def greet_c(d, carry):
        pl.semaphore_signal(barrier, inc=1, device_id=(me_s, cross(d)), device_id_type=MESH)
        return carry

    def greet_s(d, carry):
        pl.semaphore_signal(barrier, inc=1, device_id=(slab(d), me_c), device_id_type=MESH)
        return carry

    lax.fori_loop(1, N_CROSS, greet_c, 0)
    lax.fori_loop(1, N_SLAB, greet_s, 0)
    pl.semaphore_wait(barrier, N_CROSS - 1 + N_SLAB - 1)

    def remote(src, dst, sems, peer):
        return pltpu.make_async_remote_copy(
            src_ref=src,
            dst_ref=dst,
            send_sem=sems.at[0],
            recv_sem=sems.at[1],
            device_id=peer,
            device_id_type=MESH,
        )

    def drain(ref, sem):
        pltpu.make_async_copy(ref, ref, sem).wait()

    mine = jnp.zeros((8, 128), jnp.int32)
    for k in range(4):
        mine = mine + jnp.where(iota(1) == 4 * me_c + k, tg_ref[0, k], 0)
    tgv[...] = mine
    tgb[me_c] = mine

    def send_targets(d, carry):
        remote(tgv, tgb.at[me_c], tsem, (me_s, cross(d))).start()
        return carry

    lax.fori_loop(1, N_CROSS, send_targets, 0)

    def parts(g):
        at = 0
        for which, first, count in GROUPS[g]:
            yield arrays[which], first, count, at
            at += count

    def phase1(g):
        sems = p1.at[g]

        def body(d, carry):
            m = cross(d)
            for src, first, count, at in parts(g):
                remote(
                    src.at[pl.ds(first, count), m],
                    bufs[g].at[me_c, pl.ds(at, count)],
                    sems,
                    (me_s, m),
                ).start()
            return carry

        lax.fori_loop(1, N_CROSS, body, 0)
        for src, first, count, at in parts(g):
            pltpu.make_async_copy(
                src.at[pl.ds(first, count), me_c], bufs[g].at[me_c, pl.ds(at, count)], lsem.at[g]
            ).start()

    def phase2(g):
        width = WIDTHS[g]
        sems = p1.at[g]
        drain(bufs[g].at[pl.ds(0, N_CROSS - 1)], sems.at[1])
        drain(bufs[g].at[0], lsem.at[g])

        def fill(t):
            for q in range(4):
                code = inv_s[t * 4 + q, 0] & 63
                outs[g][t, :, q : q + 5 : 4, :] = bufs[g][
                    lax.div(code, 4), :, pl.ds(lax.rem(code, 4), 2, stride=4), :
                ]

        def body(d, carry):
            t = cross(d)
            fill(t)
            remote(outs[g].at[t], placed[g].at[me_c], p2.at[g], (me_s, t)).start()
            return carry

        lax.fori_loop(1, N_CROSS, body, 0)
        fill(me_c)
        pltpu.make_async_copy(outs[g].at[me_c], placed[g].at[me_c], lsem.at[g]).start()

    def landed(g):
        drain(placed[g].at[pl.ds(0, N_CROSS - 1)], p2.at[g, 1])
        drain(placed[g].at[0], lsem.at[g])

    def sent(g):
        drain(bufs[g].at[pl.ds(0, N_CROSS - 1)], p1.at[g, 0])
        drain(outs[g].at[pl.ds(0, N_CROSS - 1)], p2.at[g, 0])

    def invert():
        drain(tgb.at[pl.ds(0, N_CROSS - 1)], tsem.at[1])
        flat = tgb[0]
        for s in range(1, N_CROSS):
            flat = flat + tgb[s]
        for tile in range(8):
            hit = flat == iota(0) + 8 * tile
            code = jnp.sum(jnp.where(hit & (iota(1) < 64), iota(1), 0), axis=1, keepdims=True)
            inv_v[8 * tile : 8 * tile + 8, :] = jnp.broadcast_to(code, (8, 128))
        to_scalar = pltpu.make_async_copy(inv_v, inv_s, lsem.at[n])
        to_scalar.start()
        to_scalar.wait()

    halo = []

    def send_halos():
        x_lo = (me_s, lax.rem(me_c + N_CROSS - 1, N_CROSS))
        x_hi = (me_s, lax.rem(me_c + 1, N_CROSS))
        spans = [(0, 0, 1), (0, 3, GAS[0] - 3)] + [(g, 0, GAS[g]) for g in range(1, N_GAS)]
        for k, (g, row, count) in enumerate(spans):
            at, rows = pl.ds(sum(GAS[:g]) + row, count), pl.ds(row, count)
            halo.append(remote(placed[g].at[0, rows], xh.at[at], hsem.at[2 * k], x_lo))
            halo.append(remote(placed[g].at[BE - 1, rows], xl.at[at], hsem.at[2 * k + 1], x_hi))
        for copy in halo:
            copy.start()
        pack_z(placed, z0, z15)
        z_lo = (slab(N_SLAB - 1), me_c)
        z_hi = (slab(1), me_c)
        for copy in (
            remote(z0, zh, hsem.at[2 * N_GAS + 2], z_lo),
            remote(z15, zl, hsem.at[2 * N_GAS + 3], z_hi),
        ):
            copy.start()
            halo.append(copy)

    def parcels1(d, carry):
        c = cross(d)
        remote(sb.at[c], r1.at[me_c], psem.at[0], (me_s, c)).start()
        return carry

    def parcels2(d, carry):
        a = slab(d)
        remote(r1.at[:, a], r2.at[me_s], psem.at[1], (a, me_c)).start()
        return carry

    kept = {}
    chunks = N_SLAB * N_CROSS * CAP // CHUNK
    for name, g in SCHEDULE:
        if name == "1":
            phase1(g)
        elif name == "2":
            phase2(g)
        elif name == "landed":
            landed(g)
        elif name == "pack":
            for fetch in fetches:
                fetch.wait()
            pack(mass_ref, ps_ref, box_ref, cell_ref, count_ref, w, spans_v, spans_s, lsem.at[n], sb)
            lax.fori_loop(1, N_CROSS, parcels1, 0)
            own = pltpu.make_async_copy(sb.at[me_c], r1.at[me_c], lsem.at[n])
            own.start()
            own.wait()
        elif name == "invert":
            invert()
        elif name == "pass":
            drain(r1.at[pl.ds(0, N_CROSS - 1)], psem.at[0, 1])
            lax.fori_loop(1, N_SLAB, parcels2, 0)
            own = pltpu.make_async_copy(r1.at[:, me_s], r2.at[me_s], lsem.at[n])
            own.start()
            own.wait()
        elif name == "halo":
            send_halos()
        elif name == "faces":
            for copy in halo:
                copy.wait()
            kept["sweep"] = faces(
                d_ref, placed, xl, xh, zl, zh, z0, z15, tend_ref,
                gx, hx, gy, hy, gz, hz, gzp, hzp,
            )
        elif name == "sweep":
            kept["sweep"](g)
        elif name == "advance":
            advance(placed, g, tend_ref, new_ref)
        elif name == "parcels":
            drain(r2.at[pl.ds(0, N_SLAB - 1)], psem.at[1, 1])
            deposit_start(placed[0], r2, new_ref, vals, tabs)
            kept["acc"] = jnp.zeros((512, 128), F32)
        elif name == "chunks":
            low, high = chunks * g // 4, chunks * (g + 1) // 4
            kept["acc"] = deposit_chunks(low, high, kept["acc"], vals, tabs)
        elif name == "deposit":
            deposit_end(kept["acc"], new_ref)

    drain(tgb.at[pl.ds(0, N_CROSS - 1)], tsem.at[0])
    drain(r1.at[pl.ds(0, N_CROSS - 1)], psem.at[0, 0])
    drain(r2.at[pl.ds(0, N_SLAB - 1)], psem.at[1, 0])
    for g in range(n):
        sent(g)


def pack_z(placed, z0, z15):
    lane16 = iota(1) // 16
    upper = iota(0) >= 4

    for g in range(N_GAS):
        first = sum(GAS[:g])

        def body(f, carry):
            low = [None, None]
            high = [None, None]
            for ih in range(2):
                for il in range(8):
                    x = placed[g][ih * 8 + il, f]
                    a = lane_roll(x, 16 * il)
                    b = lane_roll(x, 16 * il + 16)
                    if il == 0:
                        low[ih], high[ih] = a, b
                    else:
                        low[ih] = jnp.where(lane16 == il, a, low[ih])
                        high[ih] = jnp.where(lane16 == il, b, high[ih])
            z0[first + f] = jnp.where(upper, sub_roll(low[1], 4), low[0])
            z15[first + f] = jnp.where(upper, high[1], sub_roll(high[0], 4))
            return carry

        lax.fori_loop(0, GAS[g], body, 0)


def step(state, velocity, history, diffusion, targets, mass, parcels, box, cell, count):
    vm = pl.BlockSpec(memory_space=pltpu.VMEM)
    sm = pl.BlockSpec(memory_space=pltpu.SMEM)
    hbm = pl.BlockSpec(memory_space=pl.ANY)
    group = [(N_CROSS, w, 8, 128) for w in WIDTHS]
    devices = N_SLAB * N_CROSS
    out = jax.ShapeDtypeStruct((FIELDS, BE, 8, 128), F32)
    return pl.pallas_call(
        step_kernel,
        out_shape=[pltpu.VMEM((FIELDS, BE, 8, 128), F32)] * 2,
        in_specs=[hbm, hbm, hbm, sm, sm, hbm, hbm, hbm, hbm, sm],
        out_specs=[vm, vm],
        scratch_shapes=[pltpu.VMEM(s, F32) for s in group * 3]
        + [pltpu.VMEM((sum(GAS), 8, 128), F32)] * 6
        + [pltpu.VMEM((N_CROSS, N_SLAB, 4, 128), F32)] * 2
        + [pltpu.VMEM((N_SLAB, N_CROSS, 4, 128), F32)]
        + [
            pltpu.VMEM((8, 128), jnp.int32),
            pltpu.VMEM((N_CROSS, 8, 128), jnp.int32),
            pltpu.VMEM((64, 128), jnp.int32),
            pltpu.SMEM((64, 128), jnp.int32),
            pltpu.VMEM((PAR_DEV // 128 + 1, 8, 128), F32),
            pltpu.VMEM((devices, 128), jnp.int32),
            pltpu.SMEM((devices, 128), jnp.int32),
        ]
        + [pltpu.VMEM((BE + 1, 8, 128), F32)] * 2
        + [pltpu.VMEM((BE, 8, 128), F32)] * 4
        + [pltpu.VMEM((2, 8, 128), F32)] * 2
        + [pltpu.VMEM((8, devices * CAP), F32), pltpu.VMEM((640, 256), BF16)]
        + [
            pltpu.SemaphoreType.DMA((2,)),
            pltpu.SemaphoreType.DMA((len(GROUPS), 2)),
            pltpu.SemaphoreType.DMA((len(GROUPS), 2)),
            pltpu.SemaphoreType.DMA((2 * N_GAS + 4, 2)),
            pltpu.SemaphoreType.DMA((2, 2)),
            pltpu.SemaphoreType.DMA((len(GROUPS) + 1,)),
            pltpu.VMEM((1, PAR_DEV), F32),
            pltpu.VMEM((5, PAR_DEV), F32),
            pltpu.VMEM((1, PAR_DEV), jnp.int32),
            pltpu.VMEM((1, PAR_DEV), jnp.int32),
            pltpu.SemaphoreType.DMA((4,)),
        ],
        compiler_params=pltpu.CompilerParams(
            collective_id=0, has_side_effects=True, vmem_limit_bytes=VMEM_LIMIT
        ),
    )(state, velocity, history, diffusion, targets, mass, parcels, box, cell, count)


def hand_over_kernel(a_ref, b_ref, a_out, b_out, sems):
    copies = []
    for k, (src, dst) in enumerate(((a_ref, a_out), (b_ref, b_out))):
        for part in range(2):
            at = pl.ds(part * (FIELDS // 2), FIELDS // 2)
            copies.append(pltpu.make_async_copy(src.at[at], dst.at[at], sems.at[2 * k + part]))
    for copy in copies:
        copy.start()
    for copy in copies:
        copy.wait()


def hand_over(a, b):
    out = jax.ShapeDtypeStruct((FIELDS, BE, 8, 128), F32)
    return pl.pallas_call(
        hand_over_kernel,
        out_shape=[out, out],
        in_specs=[pl.BlockSpec(memory_space=pl.ANY)] * 2,
        out_specs=[pl.BlockSpec(memory_space=pl.ANY)] * 2,
        scratch_shapes=[pltpu.SemaphoreType.DMA((4,))],
        compiler_params=pltpu.CompilerParams(vmem_limit_bytes=8 * 2**20),
    )(a, b)


def spread_of(e):
    return 1.0 + 0.5 * jnp.tanh(e)


def faces(
    d_ref, placed, xl, xh, zl, zh, z0, z15, tend_ref, gx, hx, gy, hy, gz, hz, gzp, hzp
):
    me_c = lax.axis_index("cross")
    lane = iota(1)
    row = iota(0)
    kl7 = lane >= 112
    kl0 = lane < 16
    top = kl7 & (row >= 4)
    bottom = kl0 & (row < 4)
    j15 = lane % 16 == 15
    j0 = lane % 16 == 0
    wall_y = j15 & (row % 4 == 3)

    def up_z(q):
        return lane_roll(jnp.where(kl0, sub_roll(q, 4), q), -16)

    def down_z(q):
        return lane_roll(jnp.where(kl7, sub_roll(q, 4), q), 16)

    def up_y(q):
        return jnp.where(j15, sub_roll(lane_roll(q, 15), -1), lane_roll(q, -1))

    def down_y(q):
        return jnp.where(j0, sub_roll(lane_roll(q, -15), 1), lane_roll(q, 1))

    def put_top(packed, i):
        ih, il = divmod(i, 8)
        return lane_roll(packed[1 - ih], 112 - 16 * il)

    def put_bottom(packed, i):
        ih, il = divmod(i, 8)
        return lane_roll(packed[ih], -16 * il)

    p0 = placed[0]
    pe, E, _ = place_of(0, FIELDS - 1)
    EH = sum(GAS[:pe]) + E
    pe = placed[pe]
    first_wall = jnp.where(me_c == 0, 0.0, 1.0)
    last_wall = jnp.where(me_c == N_CROSS - 1, 0.0, 1.0)
    before_g = spread_of(xl[EH])
    before_u = xl[0]
    for i in range(BE + 1):
        if i < BE:
            now_g, now_u = spread_of(pe[i, E]), p0[i, 0]
        else:
            now_g, now_u = spread_of(xh[EH]), xh[0]
        g, h = 0.5 * (before_g + now_g), 0.25 * (before_u + now_u)
        if i == 0:
            g, h = g * first_wall, h * first_wall
        if i == BE:
            g, h = g * last_wall, h * last_wall
        gx[i], hx[i] = g, h
        before_g, before_u = now_g, now_u
        if i < BE:
            uy, uz = p0[i, 1], p0[i, 2]
            gy[i] = jnp.where(wall_y, 0.0, 0.5 * (now_g + up_y(now_g)))
            hy[i] = jnp.where(wall_y, 0.0, 0.25 * (uy + up_y(uy)))
            gz[i] = 0.5 * (now_g + up_z(now_g))
            hz[i] = 0.25 * (uz + up_z(uz))
    gzp[0] = 0.5 * (spread_of(zl[EH]) + spread_of(z0[EH]))
    gzp[1] = 0.5 * (spread_of(z15[EH]) + spread_of(zh[EH]))
    hzp[0] = 0.25 * (zl[2] + z0[2])
    hzp[1] = 0.25 * (z15[2] + zh[2])

    def flux(d, g, h, low, high):
        return (d * g) * (high - low) - h * (high + low)

    def sweep(q_ref, q_at, x_at, out_at, count):
        def body(n, carry):
            f = out_at + n
            d = d_ref[f]
            xf = x_at + n
            qf = q_at + n
            edge0 = flux(d, gzp[0], hzp[0], zl[xf], z0[xf])
            edge15 = flux(d, gzp[1], hzp[1], z15[xf], zh[xf])
            edge0 = (edge0, sub_roll(edge0, 4))
            edge15 = (edge15, sub_roll(edge15, 4))
            q = q_ref[0, qf]
            fx = flux(d, gx[0], hx[0], xl[xf], q)
            for i in range(BE):
                ahead = q_ref[i + 1, qf] if i < BE - 1 else xh[xf]
                fx_up = flux(d, gx[i + 1], hx[i + 1], q, ahead)
                total = fx_up - fx
                fz = flux(d, gz[i], hz[i], q, up_z(q))
                fz = jnp.where(top, put_top(edge15, i), fz)
                fz_low = jnp.where(bottom, put_bottom(edge0, i), down_z(fz))
                total = total + fz - fz_low
                fy = flux(d, gy[i], hy[i], q, up_y(q))
                total = total + fy - down_y(fy)
                tend_ref[f, i] = total
                fx = fx_up
                q = ahead
            return carry

        lax.fori_loop(0, count, body, 0)

    def sweep_group(g):
        for first, count, group, row in runs(0):
            if group == g:
                sweep(placed[g], row, sum(GAS[:g]) + row, first, count)

    return sweep_group


def advance(placed, g, tend_ref, new_ref):
    for first, count, group, h_row in runs(2):
        if group != g:
            continue
        f = first
        while f < first + count:
            q_group, q_row, left = place_of(0, f)
            many = min(left, first + count - f)
            advance_run(placed[q_group], q_row, placed[g], h_row + f - first, tend_ref, new_ref, f, many)
            f += many


def advance_run(q_ref, q_at, h_ref, h_at, tend_ref, new_ref, f_at, count):
    def body(m, carry):
        new_ref[f_at + m] = q_ref[:, q_at + m] + TIME_STEP * (
            1.5 * tend_ref[f_at + m] - 0.5 * h_ref[:, h_at + m]
        )
        return carry

    lax.fori_loop(0, count, body, 0)


def deposit_start(p0, r2, new_ref, vals, tabs):
    tables = [new_ref[0], new_ref[FIELDS - 1]] + [p0[:, d] for d in range(3)]
    for n, table in enumerate(tables):
        table = table.reshape(128, 128)
        first = table.astype(BF16)
        tabs[128 * n : 128 * n + 128, 0:128] = first
        tabs[128 * n : 128 * n + 128, 128:256] = (table - first.astype(F32)).astype(BF16)

    half = iota(1, (4, 128)) < 64

    def unpack(n, carry):
        a, b = r2[n // 8, 2 * (n % 8)], r2[n // 8, 2 * (n % 8) + 1]
        at = pl.ds(pl.multiple_of(n * 128, 128), 128)
        vals[0:4, at] = jnp.where(half, a, pltpu.roll(b, 64, 1))
        vals[4:8, at] = jnp.where(half, pltpu.roll(a, 64, 1), b)
        return carry

    lax.fori_loop(0, 64, unpack, 0, unroll=4)


def deposit_chunks(low, high, acc, vals, tabs):
    number = lax.broadcasted_iota(jnp.int32, (128, CHUNK), 0).astype(F32)

    def add_chunk(n, acc):
        v = vals[:, pl.ds(pl.multiple_of(n * CHUNK, CHUNK), CHUNK)]
        at_row = number == v[3:4]
        at_lane = jnp.where(number == v[7:8], 1.0, 0.0).astype(BF16)
        picked = jnp.dot(
            tabs[...], jnp.concatenate([at_lane, at_lane], axis=0), preferred_element_type=F32
        )

        def value(m):
            return jnp.sum(
                jnp.where(at_row, picked[128 * m : 128 * m + 128], 0.0), axis=0, keepdims=True
            )

        slip = (value(2) - v[4:5]) ** 2 + (value(3) - v[5:6]) ** 2 + (value(4) - v[6:7]) ** 2
        coef = v[0:1] * jnp.sqrt(1.0 + slip)
        rate = coef * (v[1:2] - value(0))
        heat = coef * (v[2:3] - value(1)) - LATENT * rate
        rows = []
        for x in (rate, heat):
            first = x.astype(BF16).astype(F32)
            rows.append(jnp.where(at_row, first, 0.0).astype(BF16))
            rows.append(jnp.where(at_row, x - first, 0.0).astype(BF16))
        return acc + lax.dot_general(
            jnp.concatenate(rows, axis=0),
            at_lane,
            (((1,), (1,)), ((), ())),
            preferred_element_type=F32,
        )

    return lax.fori_loop(low, high, add_chunk, acc)


def deposit_end(acc, new_ref):
    fuel = (acc[0:128] + acc[128:256]).reshape(BE, 8, 128)
    heat = (acc[256:384] + acc[384:512]).reshape(BE, 8, 128)
    new_ref[0] = new_ref[0] + DEPOSIT * fuel
    new_ref[FIELDS - 1] = new_ref[FIELDS - 1] + DEPOSIT * heat


def to_tiles(array):
    fields = array.shape[0]
    return (
        array.reshape(fields, 4, 32, 128).transpose(0, 2, 1, 3).reshape(fields, BE, 8, 128)
    )


def from_tiles(array):
    fields = array.shape[0]
    return array.reshape(fields, 32, 4, 128).transpose(0, 2, 1, 3).reshape(fields, 4, 4096)


def per_device(
    state,
    velocity,
    history,
    diffusion,
    box_target,
    parcel_mass,
    parcel_state,
    parcel_box,
    parcel_cell,
    parcel_count,
):
    new_state, tendency = step(
        to_tiles(state),
        to_tiles(velocity),
        to_tiles(history),
        diffusion,
        box_target,
        parcel_mass[None],
        parcel_state,
        parcel_box[None],
        parcel_cell[None],
        parcel_count,
    )
    new_state, tendency = hand_over(new_state, tendency)
    return from_tiles(new_state), from_tiles(tendency)


def solution(mesh):
    return jax.shard_map(
        per_device,
        mesh=mesh,
        in_specs=(
            P(None, ("slab", "cross"), None),
            P(None, ("slab", "cross"), None),
            P(None, ("slab", "cross"), None),
            P(),
            P("slab", "cross"),
            P(("slab", "cross")),
            P(None, ("slab", "cross")),
            P(("slab", "cross")),
            P(("slab", "cross")),
            P(("slab", "cross")),
        ),
        out_specs=(P(None, ("slab", "cross"), None), P(None, ("slab", "cross"), None)),
        check_vma=False,
    )
```
